128 devices in a mesh: group: 2 (over x_hi), gx: 8 (over x_lo, y), yz: 8 (over z, core).
Axes of the slice: x: 4 (x_hi: 2, x_lo: 2; x = x_hi * 2 + x_lo), y: 4, z: 4, core: 2. Of those that a mesh axis runs over, the one named last changes fastest.
Arguments:
- site_pos: float32 [2, 8, 8, 3, 16384], P('group', 'gx', 'yz'), may hold values from -6 to 6
- zone_id: int32 [2, 8, 8, 16384], P('group', 'gx', 'yz'), may hold values from 0 to 2, as said below
- site_eps: float32 [2, 8, 8, 16384], P('group', 'gx', 'yz'), may hold values from 0.5 to 1.5
- site_mass: float32 [2, 8, 8, 16384], P('group', 'gx', 'yz'), may hold values from 0.5 to 8
- neighbours: int32 [2, 8, 8, 16, 2048], P('group', 'gx', 'yz'), may hold values from 0 to 20480, as said below
- ghost_rows: int32 [2, 8, 8, 16384], P('group', 'gx', 'yz'), may hold values from 0 to 16383, as said below
- hyb_map: int32 [2, 8, 8, 8, 512], P('group', 'gx', 'yz'), may hold values from 0 to 16383, as said below
Outputs:
- forces: float32 [2, 8, 8, 3, 16384], P('group', 'gx', 'yz')
The draws below stay inside these ranges and needn't reach their ends.
Inputs may be any that keep to these rules, and one draw needn't show every extreme that they name: `zone_id`: rows of group index 0 are 0 or 1, rows of group index 1 are 1 or 2. `neighbours`: each entry names a cluster tile of the device's lookup: 2048 local tiles, then nine blocks of 2048 ghost tiles by offsets along gx (outer) and yz (inner), then the padding tile at (163840) // 8. No entry names the block of offset (0, 0). `ghost_rows`: distinct rows of the device. `hyb_map`: on group index 0 all 4096 entries of a device are distinct; on group index 1 the 8 entries of a bead are equal and beads are distinct.
All inputs are finite; a program needn't handle non-finite values.
Results may differ from the reference program's by a relative error of at most 0.0003.
Values sent between devices are 32-bit elements; how exact they have to be, the bound alone decides.
A program may use at most 128 MiB of HBM per device.

```python
import math
import jax
import jax.numpy as jnp
from jax import lax

ROWS = 16384
CL = 8
NEIGH = 16
GHOSTS = 16384
HYB = 512
MEMBERS = 8
NBS = 16
BINS = 256
N_GROUP = 2
N_GX = 8
N_YZ = 8


def draw_zone_id(key, part):
    zone_bits = jax.random.randint(key, (N_GROUP, N_GX, N_YZ, ROWS), 0, 2)
    group_ids = jnp.arange(N_GROUP, dtype=jnp.int32).reshape(N_GROUP, 1, 1, 1)
    return (zone_bits + group_ids).astype(jnp.int32)


def draw_site_mass(key, part):
    row_key, device_key = jax.random.split(jax.random.fold_in(key, 11))
    row_scale = jnp.exp(jax.random.uniform(row_key, (N_GROUP, N_GX, N_YZ, ROWS), jnp.float32, math.log(0.5), math.log(2.0)))
    device_scale = jnp.exp(jax.random.uniform(device_key, (N_GROUP, N_GX, N_YZ, 1), jnp.float32, 0.0, math.log(4.0)))
    return jnp.clip(row_scale * device_scale, 0.5, 8.0).astype(jnp.float32)


def draw_neighbours(key, part):
    id_key, count_key = jax.random.split(jax.random.fold_in(key, 23))
    local_tiles = ROWS // CL
    ghost_tiles = GHOSTS // CL
    clusters = ROWS // CL
    shape = (N_GROUP, N_GX, N_YZ, NEIGH, clusters)
    raw_ids = jax.random.randint(id_key, shape, 0, local_tiles + 8 * ghost_tiles)
    middle = local_tiles + 4 * ghost_tiles
    tile_ids = jnp.where(raw_ids >= middle, raw_ids + ghost_tiles, raw_ids)
    live_count = jax.random.randint(count_key, (N_GROUP, N_GX, N_YZ, 1, clusters), NEIGH // 2, NEIGH + 1)
    live_count = live_count.at[..., 0].set(NEIGH // 2)
    slot_ids = jnp.arange(NEIGH, dtype=jnp.int32).reshape(NEIGH, 1)
    padded = jnp.where(slot_ids < live_count, tile_ids, local_tiles + 9 * ghost_tiles)
    padded = padded.at[..., 0, 0].set(0)
    return padded.astype(jnp.int32)


def draw_ghost_rows(key, part):
    device_keys = jax.random.split(jax.random.fold_in(key, 37), N_GROUP * N_GX * N_YZ)
    shuffled = jax.vmap(lambda device_key: jax.random.permutation(device_key, ROWS)[:GHOSTS])(device_keys)
    return shuffled.reshape(N_GROUP, N_GX, N_YZ, GHOSTS).astype(jnp.int32)


def draw_hyb_map(key, part):
    device_keys = jax.random.split(jax.random.fold_in(key, 41), N_GROUP * N_GX * N_YZ)
    shuffled = jax.vmap(lambda device_key: jax.random.permutation(device_key, ROWS)[:MEMBERS * HYB])(device_keys)
    shuffled = shuffled.reshape(N_GROUP, N_GX, N_YZ, MEMBERS, HYB)
    bead_rows = jnp.broadcast_to(shuffled[:, :, :, 0:1, :], shuffled.shape)
    group_ids = jnp.arange(N_GROUP, dtype=jnp.int32).reshape(N_GROUP, 1, 1, 1, 1)
    return jnp.where(group_ids == 0, shuffled, bead_rows).astype(jnp.int32)


def level_of(own_key, shape, shards, low, high):
    def one(axis_at, blocks):
        draws = jax.random.uniform(jax.random.fold_in(jax.random.fold_in(own_key, 6), axis_at), (blocks,), jnp.float32, low / len(shards), high / len(shards))
        return jnp.repeat(jnp.exp(draws), shape[axis_at] // blocks).reshape((-1,) + (1,) * (len(shape) - axis_at - 1))

    loudness = one(*shards[0])
    for cut in shards[1:]:
        loudness = loudness * one(*cut)
    return loudness


def bell_draw(stream_key, shape, scale, most, shards=(), kind=jnp.bfloat16):
    factor_of = level_of(stream_key, shape, shards, -0.22, 0.18) if shards else 1.0
    values = jax.random.normal(stream_key, shape, jnp.float32) * scale * factor_of
    return jnp.minimum(jnp.maximum(values, -most), most).astype(kind)


def setup_inputs(seed: int = 0) -> dict:
    key_list = jax.random.split(jax.random.key(seed), 8)
    return {
        "site_pos": bell_draw(key_list[0], (N_GROUP, N_GX, N_YZ, 3, ROWS), 1.0, 6.0, ((0, 2), (1, 8), (2, 8)), jnp.float32),
        "zone_id": draw_zone_id(jax.random.fold_in(key_list[7], 71), 0),
        "site_eps": jnp.clip(jnp.exp(math.log(1.5) - 1.0986123 * jax.random.uniform(key_list[2], (N_GROUP, N_GX, N_YZ, ROWS), jnp.float32) ** level_of(key_list[2], (N_GROUP, N_GX, N_YZ, ROWS), ((0, 2), (1, 8), (2, 8)), -0.2, 0.2)), 0.5, 1.5),
        "site_mass": draw_site_mass(jax.random.fold_in(key_list[7], 71), 0),
        "neighbours": draw_neighbours(jax.random.fold_in(key_list[7], 71), 0),
        "ghost_rows": draw_ghost_rows(jax.random.fold_in(key_list[7], 71), 0),
        "hyb_map": draw_hyb_map(jax.random.fold_in(key_list[7], 71), 0),
    }


def resolution(coord_x, zone_ids):
    middle = jax.nn.sigmoid(2.0 * coord_x)
    return jnp.where(zone_ids == 0, 1.0, jnp.where(zone_ids == 1, middle, 0.0)).astype(jnp.float32)


def pair_curve(squared, group_id):
    return jnp.where(group_id == 0, 1.0 / (1.0 + squared) ** 3, jnp.exp(-0.5 * squared))


def short_range(positions, charges, lookup, cluster_lists, group_id):
    rows = positions.shape[1]
    tile_rows = lookup.shape[1] // CL
    clusters = rows // CL
    tiles = jnp.transpose(lookup.reshape(4, tile_rows, CL), (0, 2, 1))
    pos_tiles = jnp.transpose(positions.reshape(3, clusters, CL), (0, 2, 1))
    charge_tiles = jnp.transpose(charges.reshape(clusters, CL), (1, 0))
    forces = jnp.zeros((3, CL, clusters), jnp.float32)
    stride = min(4, cluster_lists.shape[0])
    for begin_at in range(0, cluster_lists.shape[0], stride):
        chosen = tiles[:, :, cluster_lists[begin_at:begin_at + stride]]
        offsets = pos_tiles[:, :, None, None, :] - chosen[:3, None]
        squared = jnp.sum(offsets * offsets, axis=0)
        weights = charge_tiles[:, None, None, :] * chosen[3][None] * pair_curve(squared, group_id)
        forces = forces + jnp.sum(weights[None] * offsets, axis=(2, 3))
    return jnp.transpose(forces, (0, 2, 1)).reshape(3, rows)


def site_payload(positions, resolved, scales, members):
    centres = jnp.sum(positions[:, members], axis=1) * 0.125
    site_lam = jnp.sum(resolved[members], axis=0) * 0.125
    site_scale = jnp.sum(scales[members], axis=0) * 0.125
    return jnp.concatenate([centres, site_lam[None], site_scale[None]], axis=0)


def coupling(mine_all, others):
    site_count = mine_all.shape[1]
    block_len = min(512, site_count)

    def one_block(begin_at):
        mine_part = lax.dynamic_slice_in_dim(mine_all, begin_at, block_len, 1)
        offsets = mine_part[:3, :, None] - others[:3, None, :]
        squared = jnp.sum(offsets * offsets, axis=0)
        weights = mine_part[4][:, None] * others[4][None, :] * 0.5 * (mine_part[3][:, None] + others[3][None, :]) / (1.0 + squared) ** 2
        return jnp.sum(weights[None] * offsets, axis=2) * (4.0 / site_count)

    starts = jnp.arange(site_count // block_len, dtype=jnp.int32) * block_len
    pieces = lax.map(one_block, starts)
    return jnp.moveaxis(pieces, 0, 1).reshape(3, site_count)


def spread(forces, site_pulls, members):
    shares = jnp.broadcast_to(site_pulls[:, None, :] * 0.125, (3,) + members.shape)
    return forces.at[:, members.reshape(-1)].add(shares.reshape(3, -1))


def bin_terms(coord_part, bin_count):
    centres = (jnp.arange(bin_count, dtype=jnp.float32) + 0.5) / NBS
    gap_rows = (coord_part[:, None] - centres[None, :]) * NBS
    return jnp.exp(-0.5 * gap_rows * gap_rows), gap_rows


def density(coords, masses, bin_count):
    rows_blk = min(4096, coords.shape[0])

    def one_block(begin_at):
        coord_part = lax.dynamic_slice_in_dim(coords, begin_at, rows_blk)
        mass_part = lax.dynamic_slice_in_dim(masses, begin_at, rows_blk)
        kernel, gap_rows = bin_terms(coord_part, bin_count)
        return jnp.sum(mass_part[:, None] * kernel, axis=0)

    starts = jnp.arange(coords.shape[0] // rows_blk, dtype=jnp.int32) * rows_blk
    return jnp.sum(lax.map(one_block, starts), axis=0)


def thermo_force(coords, resolved, deviation):
    rows_blk = min(4096, coords.shape[0])

    def one_block(begin_at):
        coord_part = lax.dynamic_slice_in_dim(coords, begin_at, rows_blk)
        kernel, gap_rows = bin_terms(coord_part, deviation.shape[0])
        return jnp.sum(kernel * gap_rows * deviation[None, :], axis=1)

    starts = jnp.arange(coords.shape[0] // rows_blk, dtype=jnp.int32) * rows_blk
    pushes = lax.map(one_block, starts).reshape(-1)
    return -4.0 * resolved * (1.0 - resolved) * pushes


def reference(site_pos, zone_id, site_eps, site_mass, neighbours, ghost_rows, hyb_map):
    groups = N_GROUP
    slab_count = N_GX
    columns = N_YZ
    devices = groups * slab_count * columns
    positions = site_pos.reshape(devices, 3, ROWS)
    zone_ids = zone_id.reshape(devices, ROWS)
    scales = site_eps.reshape(devices, ROWS)
    masses = site_mass.reshape(devices, ROWS)
    row_lists = neighbours.reshape(devices, NEIGH, ROWS // CL)
    ghosts = ghost_rows.reshape(devices, GHOSTS)
    members = hyb_map.reshape(devices, MEMBERS, HYB)
    device_ids = jnp.arange(devices, dtype=jnp.int32)
    group_ids = device_ids // (slab_count * columns)
    slab_ids = (device_ids // columns) % slab_count
    resolved = resolution(positions[:, 0], zone_ids)
    charges = scales * jnp.where(group_ids[:, None] == 0, resolved, 1.0 - resolved)
    coords = (group_ids * slab_count + slab_ids).astype(jnp.float32)[:, None] + jax.nn.sigmoid(positions[:, 0])
    profile = jnp.sum(lax.map(lambda device: density(coords[device], masses[device], BINS), device_ids), axis=0)
    deviation = profile / (jnp.sum(profile) / BINS) - 1.0
    ghost_data = jax.vmap(lambda row_ids, pos_dev, charge_dev: jnp.concatenate([pos_dev[:, row_ids], charge_dev[row_ids][None]], axis=0))(ghosts, positions, charges)
    ghost_grid = ghost_data.reshape(groups, slab_count, columns, 4, GHOSTS)
    site_data = jax.vmap(site_payload)(positions, resolved, scales, members)
    partner = site_data.reshape(groups, slab_count, columns, 5, HYB)[::-1].reshape(devices, 5, HYB)

    def one_device(device):
        group_id = device // (slab_count * columns)
        slab_at = (device // columns) % slab_count
        column = device % columns
        pieces = []
        for step_x in (-1, 0, 1):
            for step_y in (-1, 0, 1):
                pieces.append(ghost_grid[group_id, (slab_at + step_x) % slab_count, (column + step_y) % columns])
        local_rows = jnp.concatenate([positions[device], charges[device][None]], axis=0)
        lookup = jnp.concatenate([local_rows] + pieces + [jnp.zeros((4, CL), jnp.float32)], axis=1)
        forces = short_range(positions[device], charges[device], lookup, row_lists[device], group_id)
        site_pulls = coupling(site_data[device], partner[device])
        forces = spread(forces, site_pulls, members[device])
        pushes = thermo_force(coords[device], resolved[device], deviation)
        return forces.at[0].add(pushes)

    result = lax.map(one_device, device_ids)
    return result.reshape(groups, slab_count, columns, 3, ROWS)
```

```python
import jax
import jax.numpy as jnp
from jax import lax
from jax.experimental import pallas as pl
from jax.experimental.pallas import tpu as pltpu
from jax.sharding import PartitionSpec as P

F32 = jnp.float32
MESH = pl.DeviceIdType.MESH
LANES = 128
PIECES = 4
NBS = 16
NEAR = NBS // 2


def iota(shape, dim):
    return lax.broadcasted_iota(jnp.int32, shape, dim)


def wide(row, rows=8):
    return jnp.broadcast_to(row, (rows, LANES))


def planes_of(pos_ref, planes):
    for k in range(3):
        for c in range(LANES):
            planes[k, c : c + 1, :] = pos_ref[k : k + 1, c * LANES : (c + 1) * LANES]


def dense_tiles(quad, out_ref, v):
    comp = (iota((8, LANES), 1) // 8) % 4
    for b in range(4):
        rolled = [quad[k] if k == b else pltpu.roll(quad[k], ((k - b) * 8) % LANES, 1) for k in range(4)]
        row = jnp.where(
            comp < 2,
            jnp.where(comp == 0, rolled[0], rolled[1]),
            jnp.where(comp == 2, rolled[2], rolled[3]),
        )
        out_ref[pl.ds(pl.multiple_of(v * 32 + b * 8, 8), 8), :] = row


def lane_pick(planes, count, ids, unroll, comps):
    hi = [i >> 7 for i in ids]
    lo = [i & 127 for i in ids]
    n = len(ids)

    def step(block, accs):
        accs = list(accs)
        for rr in range(unroll):
            r = block * unroll + rr
            same = [h == r for h in hi]
            for k in range(comps):
                src = wide(planes[k, pl.ds(r, 1), :])
                for i in range(n):
                    cand = jnp.take_along_axis(src, lo[i], axis=1)
                    accs[k * n + i] = jnp.where(same[i], cand, accs[k * n + i])
        return tuple(accs)

    zero = jnp.zeros((8, LANES), F32)
    if unroll == count:
        return step(0, (zero,) * (comps * n))
    return lax.fori_loop(0, count // unroll, step, (zero,) * (comps * n))


def prep_kernel(pos_ref, zone_ref, eps_ref, ghost_ref, pay_ref, local_ref, planes):
    group = lax.axis_index("group")
    planes_of(pos_ref, planes)

    def local(v, _):
        at = pl.ds(pl.multiple_of(v * 8, 8), 8)
        x = planes[0, at, :]
        zone = zone_ref[at, :]
        lam = jnp.where(zone == 0, 1.0, jnp.where(zone == 1, jax.nn.sigmoid(2.0 * x), 0.0))
        charge = eps_ref[at, :] * jnp.where(group == 0, lam, 1.0 - lam)
        planes[3, at, :] = charge
        dense_tiles([planes[k, at, :] for k in range(4)], local_ref, v)
        return 0

    lax.fori_loop(0, 16, local, 0)

    def ghosts(v, _):
        ids = [ghost_ref[pl.ds(pl.multiple_of(v * 16 + 8 * i, 8), 8), :] for i in range(2)]
        out = lane_pick(planes, LANES, ids, LANES, 4)
        for i in range(2):
            dense_tiles([out[k * 2 + i] for k in range(4)], pay_ref, v * 2 + i)
        return 0

    lax.fori_loop(0, 8, ghosts, 0)


def fold8(parts):
    sub = iota((8, LANES), 0)
    for bit in (1, 2, 4):
        low = (sub & bit) == 0
        parts = [
            jnp.where(low, one, two) + pltpu.roll(jnp.where(low, two, one), bit, 0)
            for one, two in zip(parts[::2], parts[1::2])
        ]
    return parts[0]


def edge_distance(t, slab, other):
    above = other > slab
    shift = jnp.where(above, (other - slab) * NBS, (slab - other - 1) * NBS).astype(F32)
    slope = jnp.where(above, -1.0, 1.0).astype(F32)
    return shift + slope * t


def weight_of(n):
    return jnp.exp(-0.5 * (n + 0.5) * (n + 0.5))


def order_of(slab, lane, row):
    k = row * LANES + lane
    slab_k = k // NBS
    n = k % NBS
    ahead = jnp.where(slab_k > slab, n, NBS - 1 - n)
    own = jnp.where(n < NEAR, NEAR + n, NBS - 1 - n)
    back = jnp.where(n < NEAR, NBS - 1 - n, n - NEAR)
    steps = jnp.where(slab_k == slab, n % NEAR, n)
    to = lane - n + jnp.where(slab_k == slab, own, ahead)
    return to, lane - n + jnp.where(slab_k == slab, back, ahead), steps


def density(planes, mass_ref, slab, sums, prof):
    def far(index, _):
        other = index + (index >= slab).astype(jnp.int32)
        accs = [jnp.zeros((8, LANES), F32)] * NBS
        for v in range(16):
            t = NBS * jax.nn.sigmoid(planes[0, v * 8 : v * 8 + 8, :])
            a = edge_distance(t, slab, other)
            q = jnp.exp(-a)
            term = mass_ref[v * 8 : v * 8 + 8, :] * jnp.exp(-0.5 * a * (a + 1.0))
            for n in range(NBS):
                accs[n] = accs[n] + term
                if n < NBS - 1:
                    term = term * q
        at = pl.multiple_of(other * NBS, NBS)
        sums[pl.ds(at, 8), :] = fold8(accs[:8])
        sums[pl.ds(at + 8, 8), :] = fold8(accs[8:])
        return 0

    lax.fori_loop(0, 15, far, 0)
    accs = [jnp.zeros((8, LANES), F32)] * NBS
    for v in range(16):
        u = NBS * jax.nn.sigmoid(planes[0, v * 8 : v * 8 + 8, :]) - NEAR
        mass = mass_ref[v * 8 : v * 8 + 8, :]
        for side, sign in ((0, 1.0), (1, -1.0)):
            q = jnp.exp(sign * u)
            term = mass * jnp.exp(-0.5 * u * (u - sign))
            for n in range(NEAR):
                accs[side * NEAR + n] = accs[side * NEAR + n] + term
                if n < NEAR - 1:
                    term = term * q
    at = pl.multiple_of(slab * NBS, NBS)
    sums[pl.ds(at, 8), :] = fold8(accs[:8])
    sums[pl.ds(at + 8, 8), :] = fold8(accs[8:])
    rows = []
    lane = iota((8, LANES), 1)
    for half in range(2):
        line = jnp.sum(sums[half * LANES : (half + 1) * LANES, :].T, axis=0, keepdims=True)
        _, source, steps = order_of(slab, lane, half)
        line = wide(line) * weight_of(steps.astype(F32))
        rows.append(jnp.take_along_axis(line, source, axis=1))
    sub = iota((8, LANES), 0)
    prof[...] = jnp.where(sub == 0, rows[0], jnp.where(sub == 1, rows[1], 0.0))


def coupling(mine, theirs, cols, pulls):
    for w in range(4):
        block = theirs[:, w * LANES : (w + 1) * LANES]
        cols[w * LANES : (w + 1) * LANES, :] = jnp.concatenate([block, jnp.zeros((LANES - 8, LANES), F32)], 0).T

    def step(r, accs):
        accs = list(accs)
        lot = cols[pl.ds(pl.multiple_of(r * 8, 8), 8), :]
        other = [jnp.broadcast_to(lot[:, k : k + 1], (8, LANES)) for k in range(5)]
        for w in range(4):
            own = [wide(mine[k : k + 1, w * LANES : (w + 1) * LANES]) for k in range(5)]
            d = [own[k] - other[k] for k in range(3)]
            near = 1.0 + (d[0] * d[0] + d[1] * d[1] + d[2] * d[2])
            weight = own[4] * other[4] * (own[3] + other[3]) / (near * near)
            for k in range(3):
                accs[w * 3 + k] = accs[w * 3 + k] + weight * d[k]
        return tuple(accs)

    accs = lax.fori_loop(0, 64, step, (jnp.zeros((8, LANES), F32),) * 12)
    for w in range(4):
        for k in range(3):
            pulls[k : k + 1, w * LANES : (w + 1) * LANES] = jnp.sum(accs[w * 3 + k], axis=0, keepdims=True) * (0.5 * 4.0 / 512)


def spread(pulls, hyb_ref, out):
    total = jnp.zeros((6 * LANES, LANES), F32)
    sub = iota((LANES, 512), 0)
    shares = []
    for k in range(3):
        share = pulls[k : k + 1, :] * 0.125
        high = share.astype(jnp.bfloat16).astype(F32)
        shares += [high, share - high]
    for m in range(8):
        rows = hyb_ref[m : m + 1, :]
        hit = jnp.broadcast_to(rows >> 7, (LANES, 512)) == sub
        lot = jnp.broadcast_to(rows & 127, (LANES, 512)) == sub
        left = jnp.concatenate([jnp.where(hit, jnp.broadcast_to(s, (LANES, 512)), 0.0).astype(jnp.bfloat16) for s in shares], 0)
        right = jnp.where(lot, 1.0, 0.0).astype(jnp.bfloat16)
        total = total + lax.dot_general(left, right, (((1,), (1,)), ((), ())), preferred_element_type=F32)
    for k in range(3):
        out[k] = total[2 * k * LANES : (2 * k + 1) * LANES] + total[(2 * k + 1) * LANES : (2 * k + 2) * LANES]


def comm_kernel(
    pay_ref, pos_ref, zone_ref, eps_ref, mass_ref, hyb_ref,
    blocks_ref, prof_ref, spread_ref,
    planes, sums, part1, part2, got1, got2, mine, theirs, cols, pulls,
    send_sem, recv_sem, s1, r1, s2, r2, ss, sr,
):
    group, slab_at, column = lax.axis_index("group"), lax.axis_index("gx"), lax.axis_index("yz")
    slab = group * 8 + slab_at

    def in_column(d):
        return (group, slab_at, lax.rem(column + d, 8))

    def across(d):
        return (lax.rem(group + d // 8, 2), lax.rem(slab_at + d % 8, 8), column)

    barrier = pltpu.get_barrier_semaphore()
    for d in range(1, 8):
        pl.semaphore_signal(barrier, inc=1, device_id=in_column(d), device_id_type=MESH)
    for d in range(1, 16):
        pl.semaphore_signal(barrier, inc=1, device_id=across(d), device_id_type=MESH)
    pl.semaphore_wait(barrier, 22)

    step = 512 // PIECES
    routes = (
        (1, None, across(1)),
        (7, None, across(7)),
        (3, None, in_column(1)),
        (5, None, in_column(7)),
        (0, 1, in_column(1)),
        (2, 1, in_column(7)),
        (6, 7, in_column(1)),
        (8, 7, in_column(7)),
    )

    def copy(index, p):
        block, source, target = routes[index]
        rows = pl.ds(p * step, step)
        src = pay_ref.at[rows] if source is None else blocks_ref.at[source, rows]
        return pltpu.make_async_remote_copy(
            src_ref=src, dst_ref=blocks_ref.at[block, rows],
            send_sem=send_sem.at[index, p], recv_sem=recv_sem.at[index, p],
            device_id=target, device_id_type=MESH,
        )

    own_copies = [(i, p) for p in range(PIECES) for i in (0, 1, 2, 3)]
    for i, p in own_copies:
        copy(i, p).start()

    planes_of(pos_ref, planes)
    density(planes, mass_ref, slab, sums, part1)

    def share1(d):
        return pltpu.make_async_remote_copy(
            src_ref=part1, dst_ref=got1.at[d], send_sem=s1.at[d], recv_sem=r1.at[d],
            device_id=in_column(d), device_id_type=MESH)

    def share2(d):
        return pltpu.make_async_remote_copy(
            src_ref=part2, dst_ref=got2.at[d], send_sem=s2.at[d], recv_sem=r2.at[d],
            device_id=across(d), device_id_type=MESH)

    for d in range(1, 8):
        share1(d).start()

    def forward(p):
        for first, lot in ((0, (4, 5)), (1, (6, 7))):
            copy(first, p).wait_recv()
            for i in lot:
                copy(i, p).start()

    forward(0)

    def resolve(v, _):
        at = pl.ds(pl.multiple_of(v * 8, 8), 8)
        zone = zone_ref[at, :]
        planes[3, at, :] = jnp.where(zone == 0, 1.0, jnp.where(zone == 1, jax.nn.sigmoid(2.0 * planes[0, at, :]), 0.0))
        planes[4, at, :] = eps_ref[at, :]
        return 0

    lax.fori_loop(0, 16, resolve, 0)
    mine[...] = jnp.zeros_like(mine)
    for w in range(4):
        ids = [hyb_ref[:, w * LANES : (w + 1) * LANES]]
        out = lane_pick(planes, LANES, ids, 32, 5)
        for k in range(5):
            mine[k : k + 1, w * LANES : (w + 1) * LANES] = jnp.sum(out[k], axis=0, keepdims=True) * 0.125
    swap = pltpu.make_async_remote_copy(
        src_ref=mine, dst_ref=theirs, send_sem=ss, recv_sem=sr, device_id=across(8), device_id_type=MESH)
    swap.start()
    forward(1)
    for d in range(1, 8):
        share1(d).wait_recv()
    total = part1[...]
    for d in range(1, 8):
        total = total + got1[d]
    part2[...] = total
    for d in range(1, 16):
        share2(d).start()
    forward(2)
    swap.wait_recv()
    coupling(mine, theirs, cols, pulls)
    forward(3)
    spread(pulls, hyb_ref, spread_ref)
    for d in range(1, 16):
        share2(d).wait_recv()
    total = part2[...]
    for d in range(1, 16):
        total = total + got2[d]
    prof_ref[...] = total
    for p in range(PIECES):
        for i in range(2, 8):
            copy(i, p).wait_recv()
    for p in range(PIECES):
        for i in range(8):
            copy(i, p).wait_send()
    for d in range(1, 8):
        share1(d).wait_send()
    for d in range(1, 16):
        share2(d).wait_send()
    swap.wait_send()


def force_kernel(
    nb_ref, local_ref, blocks_ref, prof_ref, spread_ref, pos_ref, zone_ref, eps_ref,
    out_ref,
    table, planes, turned, gathered, lot_ref, forces, push, coef_a, coef_b,
):
    group = lax.axis_index("group")
    slab = group * 8 + lax.axis_index("gx")
    planes_of(pos_ref, planes)
    lane = iota((8, LANES), 1)
    quarter = lane // 32

    def fill(source, block):
        def one(r, _):
            rows = source[pl.ds(pl.multiple_of(r * 8, 8), 8), :]
            rolled = [rows] + [pltpu.roll(rows, 32 * k, 1) for k in (1, 2, 3)]
            at = block * 2048 + (r // 4) * 128 + r % 4
            for q in range(4):
                tile = jnp.where(
                    quarter < 2,
                    jnp.where(quarter == 0, rolled[-q % 4], rolled[(1 - q) % 4]),
                    jnp.where(quarter == 2, rolled[(2 - q) % 4], rolled[(3 - q) % 4]),
                )
                table[pl.ds(at + q * 4, 8, stride=16), :] = tile
            return 0

        lax.fori_loop(0, 64, one, 0, unroll=4)

    fill(local_ref, 0)
    for block in range(9):
        if block != 4:
            fill(blocks_ref.at[block], block + 1)
    table[20480:20488, :] = jnp.zeros((8, LANES), F32)

    def resolve(v, _):
        at = pl.ds(pl.multiple_of(v * 8, 8), 8)
        zone = zone_ref[at, :]
        lam = jnp.where(zone == 0, 1.0, jnp.where(zone == 1, jax.nn.sigmoid(2.0 * planes[0, at, :]), 0.0))
        planes[3, at, :] = eps_ref[at, :] * jnp.where(group == 0, lam, 1.0 - lam)
        planes[4, at, :] = -4.0 * lam * (1.0 - lam)
        return 0

    lax.fori_loop(0, 16, resolve, 0)
    for k in range(4):
        turned[k] = planes[k].T

    profile = prof_ref[...]
    mean = jnp.sum(profile) / 256.0
    for half in range(2):
        source, _, steps = order_of(slab, lane, half)
        steps = steps.astype(F32)
        dev = wide(profile[half : half + 1, :] / mean - 1.0)
        dev = jnp.take_along_axis(dev, source, axis=1) * weight_of(steps)
        coef_a[half * LANES : (half + 1) * LANES, :] = wide(dev[0:1, :], LANES).T
        coef_b[half * LANES : (half + 1) * LANES, :] = wide((dev * steps)[0:1, :], LANES).T

    def horner(q, start, count):
        a = wide(coef_a[pl.ds(start + count - 1, 1), :])
        b = wide(coef_b[pl.ds(start + count - 1, 1), :])
        for n in range(count - 2, -1, -1):
            a = a * q + wide(coef_a[pl.ds(start + n, 1), :])
            b = b * q + wide(coef_b[pl.ds(start + n, 1), :])
        return a, b

    def thermo(v):
        at = pl.ds(pl.multiple_of(v * 8, 8), 8)
        t = NBS * jax.nn.sigmoid(planes[0, at, :])
        total = jnp.zeros((8, LANES), F32)
        for index in range(15):
            other = index + (index >= slab).astype(jnp.int32)
            dist = edge_distance(t, slab, other)
            a, b = horner(jnp.exp(-dist), other * NBS, NBS)
            part = jnp.exp(-0.5 * dist * (dist + 1.0)) * ((dist + 0.5) * a + b)
            total = total + jnp.where(other > slab, -part, part)
        u = t - NEAR
        a, b = horner(jnp.exp(u), slab * NBS, NEAR)
        total = total + jnp.exp(-0.5 * u * (u - 1.0)) * ((u - 0.5) * a - b)
        a, b = horner(jnp.exp(-u), slab * NBS + NEAR, NEAR)
        total = total + jnp.exp(-0.5 * u * (u + 1.0)) * ((u + 0.5) * a + b)
        push[at, :] = planes[4, at, :] * total

    def run(curve):
        def body(cl, _):
            own = [[wide(turned[k, pl.ds(cl * 8 + i, 1), :]) for i in range(8)] for k in range(3)]
            accs = [[jnp.zeros((8, LANES), F32)] * 8 for _ in range(3)]
            for quad in range(4):
                buf = quad % 2
                for g in range(4):
                    slot = quad * 4 + g
                    for c in range(LANES):
                        tile = nb_ref.at[pl.ds(slot * 2048 + c * 16, 16)][cl]
                        gathered[buf, c : c + 1, 32 * g : 32 * g + 32] = table[pl.ds(tile, 1), 32 * g : 32 * g + 32]
                lot = gathered[buf].T
                for g in range(4):
                    x, y, z, c = [lot[32 * g + 8 * k : 32 * g + 8 * k + 8] for k in range(4)]
                    for i in range(8):
                        dx, dy, dz = own[0][i] - x, own[1][i] - y, own[2][i] - z
                        w = c * curve(dx * dx + dy * dy + dz * dz)
                        accs[0][i] = accs[0][i] + w * dx
                        accs[1][i] = accs[1][i] + w * dy
                        accs[2][i] = accs[2][i] + w * dz
            at = pl.ds(pl.multiple_of(cl * 8, 8), 8)
            charge = turned[3, at, :]
            for k in range(3):
                forces[k, at, :] = charge * fold8(accs[k])
            thermo(cl)
            return 0

        lax.fori_loop(0, 16, body, 0)

    def soft(s):
        r = 1.0 / (1.0 + s)
        return r * r * r

    @pl.when(group == 0)
    def _():
        run(soft)

    @pl.when(group != 0)
    def _():
        run(lambda s: jnp.exp(-0.5 * s))

    for k in range(3):
        plane = forces[k].T + spread_ref[k]
        if k == 0:
            plane = plane + push[...]
        planes[k] = plane
    for k in range(3):
        for c in range(LANES):
            out_ref[k : k + 1, c * LANES : (c + 1) * LANES] = planes[k, c : c + 1, :]


VMEM = pl.BlockSpec(memory_space=pltpu.VMEM)
ANY = pl.BlockSpec(memory_space=pl.ANY)
SMEM = pl.BlockSpec(memory_space=pltpu.SMEM)


def shape(*dims):
    return jax.ShapeDtypeStruct(dims, F32)


def per_device(site_pos, zone_id, site_eps, site_mass, neighbours, ghost_rows, hyb_map):
    pos = site_pos.reshape(3, 16384)
    zone = zone_id.reshape(128, 128)
    eps = site_eps.reshape(128, 128)
    mass = site_mass.reshape(128, 128)
    lists = neighbours.reshape(32768)
    ghost = ghost_rows.reshape(128, 128)
    hyb = hyb_map.reshape(8, 512)
    pay, local = pl.pallas_call(
        prep_kernel,
        out_shape=(shape(512, 128), shape(512, 128)),
        in_specs=[VMEM] * 4,
        out_specs=(VMEM, VMEM),
        scratch_shapes=[pltpu.VMEM((4, 128, 128), F32)],
        compiler_params=pltpu.CompilerParams(vmem_limit_bytes=40 * 2**20),
        name="prep",
    )(pos, zone, eps, ghost)
    blocks, prof, extra = pl.pallas_call(
        comm_kernel,
        out_shape=(shape(9, 512, 128), shape(8, 128), shape(3, 128, 128)),
        in_specs=[ANY] + [VMEM] * 5,
        out_specs=(ANY, VMEM, VMEM),
        scratch_shapes=[
            pltpu.VMEM((5, 128, 128), F32),
            pltpu.VMEM((256, 128), F32),
            pltpu.VMEM((8, 128), F32),
            pltpu.VMEM((8, 128), F32),
            pltpu.VMEM((8, 8, 128), F32),
            pltpu.VMEM((16, 8, 128), F32),
            pltpu.VMEM((8, 512), F32),
            pltpu.VMEM((8, 512), F32),
            pltpu.VMEM((512, 128), F32),
            pltpu.VMEM((8, 512), F32),
            pltpu.SemaphoreType.DMA((8, PIECES)),
            pltpu.SemaphoreType.DMA((8, PIECES)),
            pltpu.SemaphoreType.DMA((8,)),
            pltpu.SemaphoreType.DMA((8,)),
            pltpu.SemaphoreType.DMA((16,)),
            pltpu.SemaphoreType.DMA((16,)),
            pltpu.SemaphoreType.DMA,
            pltpu.SemaphoreType.DMA,
        ],
        compiler_params=pltpu.CompilerParams(
            collective_id=0, has_side_effects=True, vmem_limit_bytes=40 * 2**20
        ),
        name="exchange",
    )(pay, pos, zone, eps, mass, hyb)
    forces = pl.pallas_call(
        force_kernel,
        out_shape=shape(3, 16384),
        in_specs=[SMEM] + [VMEM] * 7,
        out_specs=VMEM,
        scratch_shapes=[
            pltpu.VMEM((20488, 128), F32),
            pltpu.VMEM((5, 128, 128), F32),
            pltpu.VMEM((4, 128, 128), F32),
            pltpu.VMEM((2, 128, 128), F32),
            pltpu.VMEM((8, 128), F32),
            pltpu.VMEM((3, 128, 128), F32),
            pltpu.VMEM((128, 128), F32),
            pltpu.VMEM((256, 128), F32),
            pltpu.VMEM((256, 128), F32),
        ],
        compiler_params=pltpu.CompilerParams(vmem_limit_bytes=48 * 2**20),
        name="forces",
    )(lists, local, blocks, prof, extra, pos, zone, eps)
    return forces.reshape(1, 1, 1, 3, 16384)


def solution(mesh):
    return jax.shard_map(
        per_device,
        mesh=mesh,
        in_specs=(
            P("group", "gx", "yz", None, None),
            P("group", "gx", "yz", None),
            P("group", "gx", "yz", None),
            P("group", "gx", "yz", None),
            P("group", "gx", "yz", None, None),
            P("group", "gx", "yz", None),
            P("group", "gx", "yz", None, None),
        ),
        out_specs=P("group", "gx", "yz", None, None),
        check_vma=False,
    )
```

```python
import jax
import jax.numpy as jnp
from jax import lax
from jax.experimental import pallas as pl
from jax.experimental.pallas import tpu as pltpu
from jax.sharding import PartitionSpec as P

F32 = jnp.float32
MESH = pl.DeviceIdType.MESH
LANES = 128
PIECES = 4
NBS = 16
NEAR = NBS // 2


def iota(shape, dim):
    return lax.broadcasted_iota(jnp.int32, shape, dim)


def wide(row, rows=8):
    return jnp.broadcast_to(row, (rows, LANES))


def dense_tiles(quad, out_ref, v):
    comp = (iota((8, LANES), 1) // 8) % 4
    for b in range(4):
        rolled = [quad[k] if k == b else pltpu.roll(quad[k], ((k - b) * 8) % LANES, 1) for k in range(4)]
        row = jnp.where(
            comp < 2,
            jnp.where(comp == 0, rolled[0], rolled[1]),
            jnp.where(comp == 2, rolled[2], rolled[3]),
        )
        out_ref[pl.ds(pl.multiple_of(v * 32 + b * 8, 8), 8), :] = row


def lane_pick(planes, ids, beside):
    hi = [i >> 7 for i in ids]
    lo = [i & 127 for i in ids]
    out = [[jnp.zeros((8, LANES), F32)] * 4 for _ in ids]
    for r in range(LANES):
        same = [h == r for h in hi]
        for k in range(4):
            src = wide(planes[k, r : r + 1, :])
            for i in range(len(ids)):
                out[i][k] = jnp.where(same[i], jnp.take_along_axis(src, lo[i], axis=1), out[i][k])
        beside(r)
    return out


def fold8(parts):
    sub = iota((8, LANES), 0)
    for bit in (1, 2, 4):
        low = (sub & bit) == 0
        parts = [
            jnp.where(low, one, two) + pltpu.roll(jnp.where(low, two, one), bit, 0)
            for one, two in zip(parts[::2], parts[1::2])
        ]
    return parts[0]


def edge_distance(t, slab, other):
    above = other > slab
    shift = jnp.where(above, (other - slab) * NBS, (slab - other - 1) * NBS).astype(F32)
    slope = jnp.where(above, -1.0, 1.0).astype(F32)
    return shift + slope * t


def weight_of(n):
    return jnp.exp(-0.5 * (n + 0.5) * (n + 0.5))


def order_of(slab, lane, row):
    k = row * LANES + lane
    slab_k = k // NBS
    n = k % NBS
    ahead = jnp.where(slab_k > slab, n, NBS - 1 - n)
    own = jnp.where(n < NEAR, NEAR + n, NBS - 1 - n)
    back = jnp.where(n < NEAR, NBS - 1 - n, n - NEAR)
    steps = jnp.where(slab_k == slab, n % NEAR, n)
    to = lane - n + jnp.where(slab_k == slab, own, ahead)
    return to, lane - n + jnp.where(slab_k == slab, back, ahead), steps


def far_term(bins, mass, accs, slab, other, v):
    a = edge_distance(bins[v * 8 : v * 8 + 8, :], slab, other)
    q = jnp.exp(-a)
    term = mass[v * 8 : v * 8 + 8, :] * jnp.exp(-0.5 * a * (a + 1.0))
    for n in range(NBS):
        accs[n] = accs[n] + term
        if n < NBS - 1:
            term = term * q


def keep_bins(sums, slab, accs):
    at = pl.multiple_of(slab * NBS, NBS)
    sums[pl.ds(at, 8), :] = fold8(accs[:8])
    sums[pl.ds(at + 8, 8), :] = fold8(accs[8:])


def density(bins, mass, slab, sums, prof):
    accs = [jnp.zeros((8, LANES), F32)] * NBS
    for v in range(16):
        u = bins[v * 8 : v * 8 + 8, :] - NEAR
        for side, sign in ((0, 1.0), (1, -1.0)):
            q = jnp.exp(sign * u)
            term = mass[v * 8 : v * 8 + 8, :] * jnp.exp(-0.5 * u * (u - sign))
            for n in range(NEAR):
                accs[side * NEAR + n] = accs[side * NEAR + n] + term
                if n < NEAR - 1:
                    term = term * q
    keep_bins(sums, slab, accs)
    rows = []
    lane = iota((8, LANES), 1)
    for half in range(2):
        line = jnp.sum(sums[half * LANES : (half + 1) * LANES, :].T, axis=0, keepdims=True)
        _, source, steps = order_of(slab, lane, half)
        line = wide(line) * weight_of(steps.astype(F32))
        rows.append(jnp.take_along_axis(line, source, axis=1))
    sub = iota((8, LANES), 0)
    prof[...] = jnp.where(sub == 0, rows[0], jnp.where(sub == 1, rows[1], 0.0))


def site_tables(planes, tables):
    for i, k in enumerate((0, 1, 2, 4, 5)):
        turned = planes[k].T
        rest = jnp.concatenate([turned[:64], turned[64:]], axis=1)
        for part in range(3):
            term = rest.astype(jnp.bfloat16)
            tables[part, i * 64 : i * 64 + 64, :] = term
            rest = rest - term.astype(F32)


def member_sites(hyb_ref, tables, sites, m):
    rows = hyb_ref[pl.ds(m, 1), :]
    upper = ((rows >> 6) & 1) * LANES + (rows >> 7)
    hot = jnp.where(jnp.broadcast_to(upper, (256, 512)) == iota((256, 512), 0), 1.0, 0.0).astype(jnp.bfloat16)
    found = jnp.dot(tables[0], hot, preferred_element_type=F32)
    found = found + jnp.dot(tables[1], hot, preferred_element_type=F32)
    found = found + jnp.dot(tables[2], hot, preferred_element_type=F32)
    pick = jnp.broadcast_to(rows & 63, (64, 512)) == iota((64, 512), 0)
    for k in range(5):
        chosen = jnp.where(pick, found[k * 64 : k * 64 + 64], 0.0)
        total = sites[k]
        for j in range(8):
            total = total + chosen[j * 8 : j * 8 + 8]
        sites[k] = total


def coupling(mine, theirs, cols, pulls):
    for w in range(4):
        block = theirs[:, w * LANES : (w + 1) * LANES]
        cols[w * LANES : (w + 1) * LANES, :] = jnp.concatenate([block, jnp.zeros((LANES - 8, LANES), F32)], 0).T

    def step(r, accs):
        accs = list(accs)
        lot = cols[pl.ds(pl.multiple_of(r * 8, 8), 8), :]
        other = [jnp.broadcast_to(lot[:, k : k + 1], (8, LANES)) for k in range(5)]
        for w in range(4):
            own = [wide(mine[k : k + 1, w * LANES : (w + 1) * LANES]) for k in range(5)]
            d = [own[k] - other[k] for k in range(3)]
            near = 1.0 + (d[0] * d[0] + d[1] * d[1] + d[2] * d[2])
            weight = own[4] * other[4] * (own[3] + other[3]) / (near * near)
            for k in range(3):
                accs[w * 3 + k] = accs[w * 3 + k] + weight * d[k]
        return tuple(accs)

    accs = lax.fori_loop(0, 64, step, (jnp.zeros((8, LANES), F32),) * 12)
    for w in range(4):
        for k in range(3):
            pulls[k : k + 1, w * LANES : (w + 1) * LANES] = jnp.sum(accs[w * 3 + k], axis=0, keepdims=True) * (0.5 * 4.0 / 512)


def spread(pulls, hyb_ref, out):
    total = jnp.zeros((6 * LANES, LANES), F32)
    sub = iota((LANES, 512), 0)
    shares = []
    for k in range(3):
        share = pulls[k : k + 1, :] * 0.125
        high = share.astype(jnp.bfloat16).astype(F32)
        shares += [high, share - high]
    for m in range(8):
        rows = hyb_ref[m : m + 1, :]
        hit = jnp.broadcast_to(rows >> 7, (LANES, 512)) == sub
        lot = jnp.broadcast_to(rows & 127, (LANES, 512)) == sub
        left = jnp.concatenate([jnp.where(hit, jnp.broadcast_to(s, (LANES, 512)), 0.0).astype(jnp.bfloat16) for s in shares], 0)
        right = jnp.where(lot, 1.0, 0.0).astype(jnp.bfloat16)
        total = total + lax.dot_general(left, right, (((1,), (1,)), ((), ())), preferred_element_type=F32)
    for k in range(3):
        out[k] = total[2 * k * LANES : (2 * k + 1) * LANES] + total[(2 * k + 1) * LANES : (2 * k + 2) * LANES]


def comm_kernel(
    pos_hbm, zone_hbm, eps_hbm, mass_hbm, ghost_hbm, hyb_hbm,
    blocks_ref, prof_ref, spread_ref, local_ref, planes,
    zone_ref, mass_ref, ghost_ref, hyb_ref, bins, tables, sites,
    pay_ref, sums, part1, part2, got1, got2, mine, theirs, cols, pulls,
    load_sem, send_sem, recv_sem, s1, r1, s2, r2, ss, sr,
):
    group, slab_at, column = lax.axis_index("group"), lax.axis_index("gx"), lax.axis_index("yz")
    slab = group * 8 + slab_at

    loads = [
        pltpu.make_async_copy(src, dst, load_sem.at[i])
        for i, (src, dst) in enumerate((
            (pos_hbm, planes.at[0:3]), (zone_hbm, zone_ref), (eps_hbm, planes.at[5]),
            (ghost_hbm, ghost_ref), (mass_hbm, mass_ref), (hyb_hbm, hyb_ref),
        ))
    ]
    for load in loads:
        load.start()

    def in_column(d):
        return (group, slab_at, lax.rem(column + d, 8))

    def across(d):
        return (lax.rem(group + d // 8, 2), lax.rem(slab_at + d % 8, 8), column)

    barrier = pltpu.get_barrier_semaphore()
    for d in range(1, 8):
        pl.semaphore_signal(barrier, inc=1, device_id=in_column(d), device_id_type=MESH)
    for d in range(1, 16):
        pl.semaphore_signal(barrier, inc=1, device_id=across(d), device_id_type=MESH)

    step = 512 // PIECES
    routes = (
        (1, None, across(1)),
        (7, None, across(7)),
        (3, None, in_column(1)),
        (5, None, in_column(7)),
        (0, 1, in_column(1)),
        (2, 1, in_column(7)),
        (6, 7, in_column(1)),
        (8, 7, in_column(7)),
    )

    def copy(index, p):
        block, source, target = routes[index]
        rows = pl.ds(p * step, step)
        src = pay_ref.at[rows] if source is None else blocks_ref.at[source, rows]
        return pltpu.make_async_remote_copy(
            src_ref=src, dst_ref=blocks_ref.at[block, rows],
            send_sem=send_sem.at[index, p], recv_sem=recv_sem.at[index, p],
            device_id=target, device_id_type=MESH,
        )

    def share1(d):
        return pltpu.make_async_remote_copy(
            src_ref=part1, dst_ref=got1.at[d], send_sem=s1.at[d], recv_sem=r1.at[d],
            device_id=in_column(d), device_id_type=MESH)

    def share2(d):
        return pltpu.make_async_remote_copy(
            src_ref=part2, dst_ref=got2.at[d], send_sem=s2.at[d], recv_sem=r2.at[d],
            device_id=across(d), device_id_type=MESH)

    def forward(p):
        for first, lot in ((0, (4, 5)), (1, (6, 7))):
            copy(first, p).wait_recv()
            for i in lot:
                copy(i, p).start()

    for i in range(3):
        loads[i].wait()

    def resolve(v, _):
        at = pl.ds(pl.multiple_of(v * 8, 8), 8)
        zone = zone_ref[at, :]
        lam = jnp.where(zone == 0, 1.0, jnp.where(zone == 1, jax.nn.sigmoid(2.0 * planes[0, at, :]), 0.0))
        planes[3, at, :] = planes[5, at, :] * jnp.where(group == 0, lam, 1.0 - lam)
        planes[4, at, :] = lam
        bins[at, :] = NBS * jax.nn.sigmoid(planes[0, at, :])
        return 0

    lax.fori_loop(0, 16, resolve, 0, unroll=4)
    site_tables(planes, tables)
    sites[...] = jnp.zeros_like(sites)
    for i in range(3, 6):
        loads[i].wait()
    pl.semaphore_wait(barrier, 22)

    def ghosts(v, _):
        ids = [ghost_ref[pl.ds(pl.multiple_of(v * 16 + 8 * i, 8), 8), :] for i in range(2)]
        index = [v * 2, jnp.minimum(v * 2 + 1, 14)]
        other = [i + (i >= slab).astype(jnp.int32) for i in index]
        accs = [jnp.zeros((8, LANES), F32)] * NBS

        def beside(r):
            if r % 4 == 0:
                far_term(bins, mass_ref, accs, slab, other[r // 64], r // 4 % 16)
            if r % 64 == 63:
                keep_bins(sums, other[r // 64], accs)
                accs[:] = [jnp.zeros((8, LANES), F32)] * NBS

        member_sites(hyb_ref, tables, sites, v)
        out = lane_pick(planes, ids, beside)
        for i in range(2):
            dense_tiles(out[i], pay_ref, v * 2 + i)
            at = pl.ds(pl.multiple_of(v * 16 + 8 * i, 8), 8)
            dense_tiles([planes[k, at, :] for k in range(4)], local_ref, v * 2 + i)

        @pl.when(v % 2 == 1)
        def _():
            for i in range(4):
                copy(i, v // 2).start()

        @pl.when((v % 2 == 1) & (v >= 5))
        def _():
            forward(v // 2 - 2)

        return 0

    lax.fori_loop(0, 8, ghosts, 0)
    mine[...] = jnp.zeros_like(mine)
    for k in range(5):
        mine[k : k + 1, :] = jnp.sum(sites[k], axis=0, keepdims=True) * 0.125
    swap = pltpu.make_async_remote_copy(
        src_ref=mine, dst_ref=theirs, send_sem=ss, recv_sem=sr, device_id=across(8), device_id_type=MESH)
    swap.start()
    density(bins, mass_ref, slab, sums, part1)
    for d in range(1, 8):
        share1(d).start()
    forward(PIECES - 2)
    forward(PIECES - 1)
    swap.wait_recv()
    coupling(mine, theirs, cols, pulls)
    for d in range(1, 8):
        share1(d).wait_recv()
    total = part1[...]
    for d in range(1, 8):
        total = total + got1[d]
    part2[...] = total
    for d in range(1, 16):
        share2(d).start()
    spread(pulls, hyb_ref, spread_ref)
    for d in range(1, 16):
        share2(d).wait_recv()
    total = part2[...]
    for d in range(1, 16):
        total = total + got2[d]
    prof_ref[...] = total
    for p in range(PIECES):
        for i in range(2, 8):
            copy(i, p).wait_recv()
    for p in range(PIECES):
        for i in range(8):
            copy(i, p).wait_send()
    for d in range(1, 8):
        share1(d).wait_send()
    for d in range(1, 16):
        share2(d).wait_send()
    swap.wait_send()


def force_kernel(
    nb_hbm, local_ref, blocks_ref, prof_ref, spread_ref, planes,
    out_ref,
    nb_ref, table, turned, gathered, lots, forces, push, coef_a, coef_b, load_sem,
):
    group = lax.axis_index("group")
    slab = group * 8 + lax.axis_index("gx")
    load = pltpu.make_async_copy(nb_hbm, nb_ref, load_sem.at[0])
    load.start()
    lane = iota((8, LANES), 1)
    quarter = lane // 32

    def fill(source, block):
        def one(r, _):
            for u in range(16):
                rows = source[pl.ds(pl.multiple_of(r * 128 + u * 8, 8), 8), :]
                rolled = [rows] + [pltpu.roll(rows, 32 * k, 1) for k in (1, 2, 3)]
                at = block * 2048 + r * 512 + (u // 4) * 128 + u % 4
                for q in range(4):
                    tile = jnp.where(
                        quarter < 2,
                        jnp.where(quarter == 0, rolled[-q % 4], rolled[(1 - q) % 4]),
                        jnp.where(quarter == 2, rolled[(2 - q) % 4], rolled[(3 - q) % 4]),
                    )
                    table[pl.ds(at + q * 4, 8, stride=16), :] = tile
            return 0

        lax.fori_loop(0, 4, one, 0)

    fill(local_ref, 0)

    def ghost_fill(index, _):
        block = index + (index >= 4).astype(jnp.int32)
        fill(blocks_ref.at[block], block + 1)
        return 0

    lax.fori_loop(0, 8, ghost_fill, 0)
    table[20480:20488, :] = jnp.zeros((8, LANES), F32)
    for k in range(4):
        turned[k] = planes[k].T

    profile = prof_ref[...]
    mean = jnp.sum(profile) / 256.0
    for half in range(2):
        source, _, steps = order_of(slab, lane, half)
        steps = steps.astype(F32)
        dev = wide(profile[half : half + 1, :] / mean - 1.0)
        dev = jnp.take_along_axis(dev, source, axis=1) * weight_of(steps)
        coef_a[half * LANES : (half + 1) * LANES, :] = wide(dev[0:1, :], LANES).T
        coef_b[half * LANES : (half + 1) * LANES, :] = wide((dev * steps)[0:1, :], LANES).T

    def horner(q, start, count):
        a = wide(coef_a[pl.ds(start + count - 1, 1), :])
        b = wide(coef_b[pl.ds(start + count - 1, 1), :])
        for n in range(count - 2, -1, -1):
            a = a * q + wide(coef_a[pl.ds(start + n, 1), :])
            b = b * q + wide(coef_b[pl.ds(start + n, 1), :])
        return a, b

    def thermo_part(t, index):
        if index < 15:
            other = index + (index >= slab).astype(jnp.int32)
            dist = edge_distance(t, slab, other)
            a, b = horner(jnp.exp(-dist), other * NBS, NBS)
            part = jnp.exp(-0.5 * dist * (dist + 1.0)) * ((dist + 0.5) * a + b)
            return jnp.where(other > slab, -part, part)
        u = t - NEAR
        a, b = horner(jnp.exp(u), slab * NBS, NEAR)
        upper = jnp.exp(-0.5 * u * (u - 1.0)) * ((u - 0.5) * a - b)
        a, b = horner(jnp.exp(-u), slab * NBS + NEAR, NEAR)
        return upper + jnp.exp(-0.5 * u * (u + 1.0)) * ((u + 0.5) * a + b)

    def take(slot, cl):
        g = slot % 4
        for c in range(LANES):
            flat = (slot // 8) * 16384 + (c // 8) * 1024 + (slot % 8) * 128 + (c % 8) * 16
            tile = nb_ref.at[pl.ds(flat, 16)][cl]
            gathered[slot // 4, c : c + 1, 32 * g : 32 * g + 32] = table[pl.ds(tile, 1), 32 * g : 32 * g + 32]

    def pairs(curve, i, cl, slots, total):
        own = [wide(turned[k, pl.ds(cl * 8 + i, 1), :]) for k in range(3)]
        for slot in slots:
            quad, g = slot // 4, slot % 4
            at = [lots[quad, 32 * g + 8 * k : 32 * g + 8 * k + 8, :] for k in range(4)]
            d = [own[k] - at[k] for k in range(3)]
            w = at[3] * curve(d[0] * d[0] + d[1] * d[1] + d[2] * d[2])
            total = [total[k] + w * d[k] for k in range(3)]
        return total

    def keep(cl, accs):
        at = pl.ds(pl.multiple_of(cl * 8, 8), 8)
        charge = turned[3, at, :]
        for k in range(3):
            forces[k, at, :] = charge * fold8([acc[k] for acc in accs])

    def run(curve):
        zero = [jnp.zeros((8, LANES), F32)] * 3

        def body(cl, _):
            for quad in range(4):
                lots[quad] = gathered[quad].T
            before = jnp.maximum(cl - 1, 0)
            at = pl.ds(pl.multiple_of(cl * 8, 8), 8)
            t = NBS * jax.nn.sigmoid(planes[0, at, :])
            push_sum = jnp.zeros((8, LANES), F32)
            accs = [zero] * 8
            for slot in range(16):
                i, first = slot // 2, slot % 2 * 8
                accs[i] = pairs(curve, i, before, range(first, first + 8), accs[i])
                push_sum = push_sum + thermo_part(t, slot)
                take(slot, cl)
            lam = planes[4, at, :]
            push[at, :] = -4.0 * lam * (1.0 - lam) * push_sum
            keep(before, accs)
            return 0

        lax.fori_loop(0, 16, body, 0)
        for quad in range(4):
            lots[quad] = gathered[quad].T
        keep(15, [pairs(curve, i, 15, range(16), zero) for i in range(8)])

    def soft(s):
        r = 1.0 / (1.0 + s)
        return r * r * r

    gathered[...] = jnp.zeros_like(gathered)
    load.wait()

    @pl.when(group == 0)
    def _():
        run(soft)

    @pl.when(group != 0)
    def _():
        run(lambda s: jnp.exp(-0.5 * s))

    for k in range(3):
        plane = forces[k].T + spread_ref[k]
        if k == 0:
            plane = plane + push[...]
        out_ref[k] = plane


VMEM = pl.BlockSpec(memory_space=pltpu.VMEM)
ANY = pl.BlockSpec(memory_space=pl.ANY)
HBM = pl.BlockSpec(memory_space=pltpu.HBM)


def shape(*dims):
    return jax.ShapeDtypeStruct(dims, F32)


def per_device(site_pos, zone_id, site_eps, site_mass, neighbours, ghost_rows, hyb_map):
    pos = site_pos.reshape(3, 128, 128)
    zone = zone_id.reshape(128, 128)
    eps = site_eps.reshape(128, 128)
    mass = site_mass.reshape(128, 128)
    lists = neighbours.reshape(2, 8, 16, 128).transpose(0, 2, 1, 3).reshape(32768)
    ghost = ghost_rows.reshape(128, 128)
    hyb = hyb_map.reshape(8, 512)
    blocks, prof, extra, local, state = pl.pallas_call(
        comm_kernel,
        out_shape=(shape(9, 512, 128), shape(8, 128), shape(3, 128, 128), shape(512, 128), shape(6, 128, 128)),
        in_specs=[HBM] * 6,
        out_specs=(ANY, VMEM, VMEM, VMEM, VMEM),
        scratch_shapes=[
            pltpu.VMEM((128, 128), jnp.int32),
            pltpu.VMEM((128, 128), F32),
            pltpu.VMEM((128, 128), jnp.int32),
            pltpu.VMEM((8, 512), jnp.int32),
            pltpu.VMEM((128, 128), F32),
            pltpu.VMEM((3, 320, 256), jnp.bfloat16),
            pltpu.VMEM((5, 8, 512), F32),
            pltpu.VMEM((512, 128), F32),
            pltpu.VMEM((256, 128), F32),
            pltpu.VMEM((8, 128), F32),
            pltpu.VMEM((8, 128), F32),
            pltpu.VMEM((8, 8, 128), F32),
            pltpu.VMEM((16, 8, 128), F32),
            pltpu.VMEM((8, 512), F32),
            pltpu.VMEM((8, 512), F32),
            pltpu.VMEM((512, 128), F32),
            pltpu.VMEM((8, 512), F32),
            pltpu.SemaphoreType.DMA((6,)),
            pltpu.SemaphoreType.DMA((8, PIECES)),
            pltpu.SemaphoreType.DMA((8, PIECES)),
            pltpu.SemaphoreType.DMA((8,)),
            pltpu.SemaphoreType.DMA((8,)),
            pltpu.SemaphoreType.DMA((16,)),
            pltpu.SemaphoreType.DMA((16,)),
            pltpu.SemaphoreType.DMA,
            pltpu.SemaphoreType.DMA,
        ],
        compiler_params=pltpu.CompilerParams(
            collective_id=0, has_side_effects=True, vmem_limit_bytes=62 * 2**20
        ),
        name="exchange",
    )(pos, zone, eps, mass, ghost, hyb)
    forces = pl.pallas_call(
        force_kernel,
        out_shape=shape(3, 128, 128),
        in_specs=[HBM, VMEM, VMEM, VMEM, VMEM, VMEM],
        out_specs=VMEM,
        scratch_shapes=[
            pltpu.SMEM((32768,), jnp.int32),
            pltpu.VMEM((20488, 128), F32),
            pltpu.VMEM((4, 128, 128), F32),
            pltpu.VMEM((4, 128, 128), F32),
            pltpu.VMEM((4, 128, 128), F32),
            pltpu.VMEM((3, 128, 128), F32),
            pltpu.VMEM((128, 128), F32),
            pltpu.VMEM((256, 128), F32),
            pltpu.VMEM((256, 128), F32),
            pltpu.SemaphoreType.DMA((1,)),
        ],
        compiler_params=pltpu.CompilerParams(vmem_limit_bytes=56 * 2**20),
        name="forces",
    )(lists, local, blocks, prof, extra, state)
    return forces.reshape(1, 1, 1, 3, 16384)


def solution(mesh):
    return jax.shard_map(
        per_device,
        mesh=mesh,
        in_specs=(
            P("group", "gx", "yz", None, None),
            P("group", "gx", "yz", None),
            P("group", "gx", "yz", None),
            P("group", "gx", "yz", None),
            P("group", "gx", "yz", None, None),
            P("group", "gx", "yz", None),
            P("group", "gx", "yz", None, None),
        ),
        out_specs=P("group", "gx", "yz", None, None),
        check_vma=False,
    )
```

```python
import jax
import jax.numpy as jnp
from jax import lax
from jax.experimental import pallas as pl
from jax.experimental.pallas import tpu as pltpu
from jax.sharding import PartitionSpec as P

F32 = jnp.float32
MESH = pl.DeviceIdType.MESH
LANES = 128
PIECES = 4
NBS = 16
NEAR = NBS // 2


def iota(shape, dim):
    return lax.broadcasted_iota(jnp.int32, shape, dim)


def wide(row, rows=8):
    return jnp.broadcast_to(row, (rows, LANES))


def dense_tiles(quad, out_ref, v):
    comp = (iota((8, LANES), 1) // 8) % 4
    for b in range(4):
        rolled = [quad[k] if k == b else pltpu.roll(quad[k], ((k - b) * 8) % LANES, 1) for k in range(4)]
        row = jnp.where(
            comp < 2,
            jnp.where(comp == 0, rolled[0], rolled[1]),
            jnp.where(comp == 2, rolled[2], rolled[3]),
        )
        out_ref[pl.ds(pl.multiple_of(v * 32 + b * 8, 8), 8), :] = row


def lane_pick(planes, ids, beside):
    hi = [i >> 7 for i in ids]
    lo = [i & 127 for i in ids]
    out = [[jnp.zeros((8, LANES), F32)] * 4 for _ in ids]
    for r in range(LANES):
        same = [h == r for h in hi]
        for k in range(4):
            src = wide(planes[k, r : r + 1, :])
            for i in range(len(ids)):
                out[i][k] = jnp.where(same[i], jnp.take_along_axis(src, lo[i], axis=1), out[i][k])
        beside(r)
    return out


def fold8(parts):
    sub = iota((8, LANES), 0)
    for bit in (1, 2, 4):
        low = (sub & bit) == 0
        parts = [
            jnp.where(low, one, two) + pltpu.roll(jnp.where(low, two, one), bit, 0)
            for one, two in zip(parts[::2], parts[1::2])
        ]
    return parts[0]


def edge_distance(t, slab, other):
    above = other > slab
    shift = jnp.where(above, (other - slab) * NBS, (slab - other - 1) * NBS).astype(F32)
    slope = jnp.where(above, -1.0, 1.0).astype(F32)
    return shift + slope * t


def weight_of(n):
    return jnp.exp(-0.5 * (n + 0.5) * (n + 0.5))


def order_of(slab, lane, row):
    k = row * LANES + lane
    slab_k = k // NBS
    n = k % NBS
    ahead = jnp.where(slab_k > slab, n, NBS - 1 - n)
    own = jnp.where(n < NEAR, NEAR + n, NBS - 1 - n)
    back = jnp.where(n < NEAR, NBS - 1 - n, n - NEAR)
    steps = jnp.where(slab_k == slab, n % NEAR, n)
    to = lane - n + jnp.where(slab_k == slab, own, ahead)
    return to, lane - n + jnp.where(slab_k == slab, back, ahead), steps


def far_term(bins, mass, accs, slab, other, v):
    a = edge_distance(bins[v * 8 : v * 8 + 8, :], slab, other)
    q = jnp.exp(-a)
    term = mass[v * 8 : v * 8 + 8, :] * jnp.exp(-0.5 * a * (a + 1.0))
    for n in range(NBS):
        accs[n] = accs[n] + term
        if n < NBS - 1:
            term = term * q


def keep_bins(sums, slab, accs):
    at = pl.multiple_of(slab * NBS, NBS)
    sums[pl.ds(at, 8), :] = fold8(accs[:8])
    sums[pl.ds(at + 8, 8), :] = fold8(accs[8:])


def density(bins, mass, slab, sums, prof):
    accs = [jnp.zeros((8, LANES), F32)] * NBS
    for v in range(16):
        u = bins[v * 8 : v * 8 + 8, :] - NEAR
        for side, sign in ((0, 1.0), (1, -1.0)):
            q = jnp.exp(sign * u)
            term = mass[v * 8 : v * 8 + 8, :] * jnp.exp(-0.5 * u * (u - sign))
            for n in range(NEAR):
                accs[side * NEAR + n] = accs[side * NEAR + n] + term
                if n < NEAR - 1:
                    term = term * q
    keep_bins(sums, slab, accs)
    rows = []
    lane = iota((8, LANES), 1)
    for half in range(2):
        line = jnp.sum(sums[half * LANES : (half + 1) * LANES, :].T, axis=0, keepdims=True)
        _, source, steps = order_of(slab, lane, half)
        line = wide(line) * weight_of(steps.astype(F32))
        rows.append(jnp.take_along_axis(line, source, axis=1))
    sub = iota((8, LANES), 0)
    prof[...] = jnp.where(sub == 0, rows[0], jnp.where(sub == 1, rows[1], 0.0))


def site_tables(planes, tables):
    for i, k in enumerate((0, 1, 2, 4, 5)):
        turned = planes[k].T
        rest = jnp.concatenate([turned[:64], turned[64:]], axis=1)
        for part in range(3):
            term = rest.astype(jnp.bfloat16)
            tables[part, i * 64 : i * 64 + 64, :] = term
            rest = rest - term.astype(F32)


def member_sites(hyb_ref, tables, sites, m):
    rows = hyb_ref[pl.ds(m, 1), :]
    upper = ((rows >> 6) & 1) * LANES + (rows >> 7)
    hot = jnp.where(jnp.broadcast_to(upper, (256, 512)) == iota((256, 512), 0), 1.0, 0.0).astype(jnp.bfloat16)
    found = jnp.dot(tables[0], hot, preferred_element_type=F32)
    found = found + jnp.dot(tables[1], hot, preferred_element_type=F32)
    found = found + jnp.dot(tables[2], hot, preferred_element_type=F32)
    pick = jnp.broadcast_to(rows & 63, (64, 512)) == iota((64, 512), 0)
    for k in range(5):
        chosen = jnp.where(pick, found[k * 64 : k * 64 + 64], 0.0)
        total = sites[k]
        for j in range(8):
            total = total + chosen[j * 8 : j * 8 + 8]
        sites[k] = total


def coupling(mine, theirs, cols, pulls):
    for w in range(4):
        block = theirs[:, w * LANES : (w + 1) * LANES]
        cols[w * LANES : (w + 1) * LANES, :] = jnp.concatenate([block, jnp.zeros((LANES - 8, LANES), F32)], 0).T

    def step(r, accs):
        accs = list(accs)
        lot = cols[pl.ds(pl.multiple_of(r * 8, 8), 8), :]
        other = [jnp.broadcast_to(lot[:, k : k + 1], (8, LANES)) for k in range(5)]
        for w in range(4):
            own = [wide(mine[k : k + 1, w * LANES : (w + 1) * LANES]) for k in range(5)]
            d = [own[k] - other[k] for k in range(3)]
            near = 1.0 + (d[0] * d[0] + d[1] * d[1] + d[2] * d[2])
            weight = own[4] * other[4] * (own[3] + other[3]) / (near * near)
            for k in range(3):
                accs[w * 3 + k] = accs[w * 3 + k] + weight * d[k]
        return tuple(accs)

    accs = lax.fori_loop(0, 64, step, (jnp.zeros((8, LANES), F32),) * 12, unroll=8)
    for w in range(4):
        for k in range(3):
            pulls[k : k + 1, w * LANES : (w + 1) * LANES] = jnp.sum(accs[w * 3 + k], axis=0, keepdims=True) * (0.5 * 4.0 / 512)


def spread(pulls, hyb_ref, out):
    total = jnp.zeros((6 * LANES, LANES), F32)
    sub = iota((LANES, 512), 0)
    shares = []
    for k in range(3):
        share = pulls[k : k + 1, :] * 0.125
        high = share.astype(jnp.bfloat16).astype(F32)
        for part in (high, share - high):
            shares.append(jnp.broadcast_to(part, (LANES, 512)).astype(jnp.bfloat16))
    for m in range(8):
        rows = hyb_ref[m : m + 1, :]
        hit = jnp.broadcast_to(rows >> 7, (LANES, 512)) == sub
        lot = jnp.broadcast_to(rows & 127, (LANES, 512)) == sub
        hot = jnp.where(hit, 1.0, 0.0).astype(jnp.bfloat16)
        left = jnp.concatenate([hot * s for s in shares], 0)
        right = jnp.where(lot, 1.0, 0.0).astype(jnp.bfloat16)
        total = total + lax.dot_general(left, right, (((1,), (1,)), ((), ())), preferred_element_type=F32)
    for k in range(3):
        out[k] = total[2 * k * LANES : (2 * k + 1) * LANES] + total[(2 * k + 1) * LANES : (2 * k + 2) * LANES]


def comm_kernel(
    pos_hbm, zone_hbm, eps_hbm, mass_hbm, ghost_hbm, hyb_hbm, list_hbm,
    blocks_ref, prof_ref, spread_ref, local_ref, planes, rows_ref,
    zone_ref, mass_ref, ghost_ref, hyb_ref, bins, tables, sites,
    pay_ref, sums, part1, part2, got1, got2, mine, theirs, cols, pulls,
    load_sem, send_sem, recv_sem, s1, r1, s2, r2, ss, sr,
):
    group, slab_at, column = lax.axis_index("group"), lax.axis_index("gx"), lax.axis_index("yz")
    slab = group * 8 + slab_at

    loads = [
        pltpu.make_async_copy(src, dst, load_sem.at[i])
        for i, (src, dst) in enumerate((
            (pos_hbm, planes.at[0:3]), (zone_hbm, zone_ref), (eps_hbm, planes.at[5]),
            (ghost_hbm, ghost_ref), (mass_hbm, mass_ref), (hyb_hbm, hyb_ref), (list_hbm, rows_ref),
        ))
    ]
    for load in loads:
        load.start()

    def in_column(d):
        return (group, slab_at, lax.rem(column + d, 8))

    def across(d):
        return (lax.rem(group + d // 8, 2), lax.rem(slab_at + d % 8, 8), column)

    barrier = pltpu.get_barrier_semaphore()
    for d in range(1, 8):
        pl.semaphore_signal(barrier, inc=1, device_id=in_column(d), device_id_type=MESH)
    for d in range(1, 16):
        pl.semaphore_signal(barrier, inc=1, device_id=across(d), device_id_type=MESH)

    step = 512 // PIECES
    routes = (
        (1, None, across(1)),
        (7, None, across(7)),
        (3, None, in_column(1)),
        (5, None, in_column(7)),
        (0, 1, in_column(1)),
        (2, 1, in_column(7)),
        (6, 7, in_column(1)),
        (8, 7, in_column(7)),
    )

    def copy(index, p):
        block, source, target = routes[index]
        rows = pl.ds(p * step, step)
        src = pay_ref.at[rows] if source is None else blocks_ref.at[source, rows]
        return pltpu.make_async_remote_copy(
            src_ref=src, dst_ref=blocks_ref.at[block, rows],
            send_sem=send_sem.at[index, p], recv_sem=recv_sem.at[index, p],
            device_id=target, device_id_type=MESH,
        )

    def share1(d):
        return pltpu.make_async_remote_copy(
            src_ref=part1, dst_ref=got1.at[d], send_sem=s1.at[d], recv_sem=r1.at[d],
            device_id=in_column(d), device_id_type=MESH)

    def share2(d):
        return pltpu.make_async_remote_copy(
            src_ref=part2, dst_ref=got2.at[d], send_sem=s2.at[d], recv_sem=r2.at[d],
            device_id=across(d), device_id_type=MESH)

    def forward(p):
        for first, lot in ((0, (4, 5)), (1, (6, 7))):
            copy(first, p).wait_recv()
            for i in lot:
                copy(i, p).start()

    for i in range(3):
        loads[i].wait()

    def resolve(v, _):
        at = pl.ds(pl.multiple_of(v * 8, 8), 8)
        zone = zone_ref[at, :]
        lam = jnp.where(zone == 0, 1.0, jnp.where(zone == 1, jax.nn.sigmoid(2.0 * planes[0, at, :]), 0.0))
        planes[3, at, :] = planes[5, at, :] * jnp.where(group == 0, lam, 1.0 - lam)
        planes[4, at, :] = lam
        bins[at, :] = NBS * jax.nn.sigmoid(planes[0, at, :])
        return 0

    lax.fori_loop(0, 16, resolve, 0, unroll=4)
    site_tables(planes, tables)
    sites[...] = jnp.zeros_like(sites)
    for i in range(3, 6):
        loads[i].wait()
    pl.semaphore_wait(barrier, 22)

    def ghosts(v, _):
        ids = [ghost_ref[pl.ds(pl.multiple_of(v * 16 + 8 * i, 8), 8), :] for i in range(2)]
        index = [v * 2, jnp.minimum(v * 2 + 1, 14)]
        other = [i + (i >= slab).astype(jnp.int32) for i in index]
        accs = [jnp.zeros((8, LANES), F32)] * NBS

        def beside(r):
            if r % 4 == 0:
                far_term(bins, mass_ref, accs, slab, other[r // 64], r // 4 % 16)
            if r % 64 == 63:
                keep_bins(sums, other[r // 64], accs)
                accs[:] = [jnp.zeros((8, LANES), F32)] * NBS

        member_sites(hyb_ref, tables, sites, v)
        out = lane_pick(planes, ids, beside)
        for i in range(2):
            dense_tiles(out[i], pay_ref, v * 2 + i)
            at = pl.ds(pl.multiple_of(v * 16 + 8 * i, 8), 8)
            dense_tiles([planes[k, at, :] for k in range(4)], local_ref, v * 2 + i)

        @pl.when(v % 2 == 1)
        def _():
            for i in range(4):
                copy(i, v // 2).start()

        @pl.when((v % 2 == 1) & (v >= 5))
        def _():
            forward(v // 2 - 2)

        return 0

    lax.fori_loop(0, 8, ghosts, 0)
    loads[6].wait()
    tile = rows_ref[...]
    rows_ref[...] = (tile & -128) | ((tile & 3) << 5) | (((tile >> 2) & 3) << 3) | ((tile >> 4) & 7)
    mine[...] = jnp.zeros_like(mine)
    for k in range(5):
        mine[k : k + 1, :] = jnp.sum(sites[k], axis=0, keepdims=True) * 0.125
    swap = pltpu.make_async_remote_copy(
        src_ref=mine, dst_ref=theirs, send_sem=ss, recv_sem=sr, device_id=across(8), device_id_type=MESH)
    swap.start()
    density(bins, mass_ref, slab, sums, part1)
    for d in range(1, 8):
        share1(d).start()
    forward(PIECES - 2)
    swap.wait_recv()
    coupling(mine, theirs, cols, pulls)
    forward(PIECES - 1)
    for d in range(1, 8):
        share1(d).wait_recv()
    total = part1[...]
    for d in range(1, 8):
        total = total + got1[d]
    part2[...] = total
    for d in range(1, 16):
        share2(d).start()
    spread(pulls, hyb_ref, spread_ref)
    for d in range(1, 16):
        share2(d).wait_recv()
    total = part2[...]
    for d in range(1, 16):
        total = total + got2[d]
    prof_ref[...] = total
    for p in range(PIECES):
        for i in range(2, 8):
            copy(i, p).wait_recv()
    for p in range(PIECES):
        for i in range(8):
            copy(i, p).wait_send()
    for d in range(1, 8):
        share1(d).wait_send()
    for d in range(1, 16):
        share2(d).wait_send()
    swap.wait_send()


def force_kernel(
    nb_hbm, local_ref, blocks_ref, prof_ref, spread_ref, planes,
    out_ref,
    nb_ref, table, turned, gathered, lots, forces, push, coef_a, coef_b, load_sem,
):
    group = lax.axis_index("group")
    slab = group * 8 + lax.axis_index("gx")
    load = pltpu.make_async_copy(nb_hbm, nb_ref, load_sem.at[0])
    load.start()
    lane = iota((8, LANES), 1)
    quarter = lane // 32

    def fill(source, block):
        def one(r, _):
            for u in range(16):
                rows = source[pl.ds(pl.multiple_of(r * 128 + u * 8, 8), 8), :]
                rolled = [rows] + [pltpu.roll(rows, 32 * k, 1) for k in (1, 2, 3)]
                at = pl.multiple_of(block * 2048 + r * 512 + u * 32, 8)
                for q in range(4):
                    tile = jnp.where(
                        quarter < 2,
                        jnp.where(quarter == 0, rolled[-q % 4], rolled[(1 - q) % 4]),
                        jnp.where(quarter == 2, rolled[(2 - q) % 4], rolled[(3 - q) % 4]),
                    )
                    table[pl.ds(at + q * 8, 8), :] = tile
            return 0

        lax.fori_loop(0, 4, one, 0)

    fill(local_ref, 0)

    def ghost_fill(index, _):
        block = index + (index >= 4).astype(jnp.int32)
        fill(blocks_ref.at[block], block + 1)
        return 0

    lax.fori_loop(0, 8, ghost_fill, 0)
    table[20480:20488, :] = jnp.zeros((8, LANES), F32)
    for k in range(4):
        turned[k] = planes[k].T

    profile = prof_ref[...]
    mean = jnp.sum(profile) / 256.0
    for half in range(2):
        source, _, steps = order_of(slab, lane, half)
        steps = steps.astype(F32)
        dev = wide(profile[half : half + 1, :] / mean - 1.0)
        dev = jnp.take_along_axis(dev, source, axis=1) * weight_of(steps)
        coef_a[half * LANES : (half + 1) * LANES, :] = wide(dev[0:1, :], LANES).T
        coef_b[half * LANES : (half + 1) * LANES, :] = wide((dev * steps)[0:1, :], LANES).T

    def horner(q, start, count):
        a = wide(coef_a[pl.ds(start + count - 1, 1), :])
        b = wide(coef_b[pl.ds(start + count - 1, 1), :])
        for n in range(count - 2, -1, -1):
            a = a * q + wide(coef_a[pl.ds(start + n, 1), :])
            b = b * q + wide(coef_b[pl.ds(start + n, 1), :])
        return a, b

    def thermo_part(t, index):
        if index < 15:
            other = index + (index >= slab).astype(jnp.int32)
            dist = edge_distance(t, slab, other)
            a, b = horner(jnp.exp(-dist), other * NBS, NBS)
            part = jnp.exp(-0.5 * dist * (dist + 1.0)) * ((dist + 0.5) * a + b)
            return jnp.where(other > slab, -part, part)
        u = t - NEAR
        a, b = horner(jnp.exp(u), slab * NBS, NEAR)
        upper = jnp.exp(-0.5 * u * (u - 1.0)) * ((u - 0.5) * a - b)
        a, b = horner(jnp.exp(-u), slab * NBS + NEAR, NEAR)
        return upper + jnp.exp(-0.5 * u * (u + 1.0)) * ((u + 0.5) * a + b)

    def take(slot, cl):
        g = slot % 4
        for c in range(LANES):
            flat = (slot // 8) * 16384 + (c // 8) * 1024 + (slot % 8) * 128 + (c % 8) * 16
            tile = nb_ref.at[pl.ds(flat, 16)][cl]
            gathered[slot // 4, c : c + 1, 32 * g : 32 * g + 32] = table[pl.ds(tile, 1), 32 * g : 32 * g + 32]

    def pairs(curve, i, cl, slots, total):
        own = [wide(turned[k, pl.ds(cl * 8 + i, 1), :]) for k in range(3)]
        for slot in slots:
            quad, g = slot // 4, slot % 4
            at = [lots[quad, 32 * g + 8 * k : 32 * g + 8 * k + 8, :] for k in range(4)]
            d = [own[k] - at[k] for k in range(3)]
            w = at[3] * curve(d[0] * d[0] + d[1] * d[1] + d[2] * d[2])
            total = [total[k] + w * d[k] for k in range(3)]
        return total

    def keep(cl, accs):
        at = pl.ds(pl.multiple_of(cl * 8, 8), 8)
        charge = turned[3, at, :]
        for k in range(3):
            forces[k, at, :] = charge * fold8([acc[k] for acc in accs])

    def run(curve):
        zero = [jnp.zeros((8, LANES), F32)] * 3

        def body(cl, _):
            for quad in range(4):
                lots[quad] = gathered[quad].T
            before = jnp.maximum(cl - 1, 0)
            at = pl.ds(pl.multiple_of(cl * 8, 8), 8)
            t = NBS * jax.nn.sigmoid(planes[0, at, :])
            push_sum = jnp.zeros((8, LANES), F32)
            accs = [zero] * 8
            for slot in range(16):
                i, first = slot // 2, slot % 2 * 8
                accs[i] = pairs(curve, i, before, range(first, first + 8), accs[i])
                push_sum = push_sum + thermo_part(t, slot)
                take(slot, cl)
            lam = planes[4, at, :]
            push[at, :] = -4.0 * lam * (1.0 - lam) * push_sum
            keep(before, accs)
            return 0

        lax.fori_loop(0, 16, body, 0)
        for quad in range(4):
            lots[quad] = gathered[quad].T
        keep(15, [pairs(curve, i, 15, range(16), zero) for i in range(8)])

    def soft(s):
        near = 1.0 + s
        r = pl.reciprocal(near, approx=True)
        r = r * (2.0 - near * r)
        return r * r * r

    gathered[...] = jnp.zeros_like(gathered)
    load.wait()

    @pl.when(group == 0)
    def _():
        run(soft)

    @pl.when(group != 0)
    def _():
        run(lambda s: jnp.exp(-0.5 * s))

    for k in range(3):
        plane = forces[k].T + spread_ref[k]
        if k == 0:
            plane = plane + push[...]
        out_ref[k] = plane


VMEM = pl.BlockSpec(memory_space=pltpu.VMEM)
ANY = pl.BlockSpec(memory_space=pl.ANY)
HBM = pl.BlockSpec(memory_space=pltpu.HBM)


def shape(*dims):
    return jax.ShapeDtypeStruct(dims, F32)


def per_device(site_pos, zone_id, site_eps, site_mass, neighbours, ghost_rows, hyb_map):
    pos = site_pos.reshape(3, 128, 128)
    zone = zone_id.reshape(128, 128)
    eps = site_eps.reshape(128, 128)
    mass = site_mass.reshape(128, 128)
    lists = neighbours.reshape(2, 8, 16, 128).transpose(0, 2, 1, 3).reshape(256, 128)
    ghost = ghost_rows.reshape(128, 128)
    hyb = hyb_map.reshape(8, 512)
    blocks, prof, extra, local, state, rows = pl.pallas_call(
        comm_kernel,
        out_shape=(shape(9, 512, 128), shape(8, 128), shape(3, 128, 128), shape(512, 128), shape(6, 128, 128), jax.ShapeDtypeStruct((256, 128), jnp.int32)),
        in_specs=[HBM] * 7,
        out_specs=(ANY, VMEM, VMEM, VMEM, VMEM, VMEM),
        scratch_shapes=[
            pltpu.VMEM((128, 128), jnp.int32),
            pltpu.VMEM((128, 128), F32),
            pltpu.VMEM((128, 128), jnp.int32),
            pltpu.VMEM((8, 512), jnp.int32),
            pltpu.VMEM((128, 128), F32),
            pltpu.VMEM((3, 320, 256), jnp.bfloat16),
            pltpu.VMEM((5, 8, 512), F32),
            pltpu.VMEM((512, 128), F32),
            pltpu.VMEM((256, 128), F32),
            pltpu.VMEM((8, 128), F32),
            pltpu.VMEM((8, 128), F32),
            pltpu.VMEM((8, 8, 128), F32),
            pltpu.VMEM((16, 8, 128), F32),
            pltpu.VMEM((8, 512), F32),
            pltpu.VMEM((8, 512), F32),
            pltpu.VMEM((512, 128), F32),
            pltpu.VMEM((8, 512), F32),
            pltpu.SemaphoreType.DMA((7,)),
            pltpu.SemaphoreType.DMA((8, PIECES)),
            pltpu.SemaphoreType.DMA((8, PIECES)),
            pltpu.SemaphoreType.DMA((8,)),
            pltpu.SemaphoreType.DMA((8,)),
            pltpu.SemaphoreType.DMA((16,)),
            pltpu.SemaphoreType.DMA((16,)),
            pltpu.SemaphoreType.DMA,
            pltpu.SemaphoreType.DMA,
        ],
        compiler_params=pltpu.CompilerParams(
            collective_id=0, has_side_effects=True, vmem_limit_bytes=62 * 2**20
        ),
        name="exchange",
    )(pos, zone, eps, mass, ghost, hyb, lists)
    forces = pl.pallas_call(
        force_kernel,
        out_shape=shape(3, 128, 128),
        in_specs=[HBM, VMEM, VMEM, VMEM, VMEM, VMEM],
        out_specs=VMEM,
        scratch_shapes=[
            pltpu.SMEM((32768,), jnp.int32),
            pltpu.VMEM((20488, 128), F32),
            pltpu.VMEM((4, 128, 128), F32),
            pltpu.VMEM((4, 128, 128), F32),
            pltpu.VMEM((4, 128, 128), F32),
            pltpu.VMEM((3, 128, 128), F32),
            pltpu.VMEM((128, 128), F32),
            pltpu.VMEM((256, 128), F32),
            pltpu.VMEM((256, 128), F32),
            pltpu.SemaphoreType.DMA((1,)),
        ],
        compiler_params=pltpu.CompilerParams(vmem_limit_bytes=56 * 2**20),
        name="forces",
    )(rows.reshape(32768), local, blocks, prof, extra, state)
    return forces.reshape(1, 1, 1, 3, 16384)


def solution(mesh):
    return jax.shard_map(
        per_device,
        mesh=mesh,
        in_specs=(
            P("group", "gx", "yz", None, None),
            P("group", "gx", "yz", None),
            P("group", "gx", "yz", None),
            P("group", "gx", "yz", None),
            P("group", "gx", "yz", None, None),
            P("group", "gx", "yz", None),
            P("group", "gx", "yz", None, None),
        ),
        out_specs=P("group", "gx", "yz", None, None),
        check_vma=False,
    )
```

```python
import jax
import jax.numpy as jnp
from jax import lax
from jax.experimental import pallas as pl
from jax.experimental.pallas import tpu as pltpu
from jax.sharding import PartitionSpec as P

F32 = jnp.float32
MESH = pl.DeviceIdType.MESH
LANES = 128
PIECES = 4
NBS = 16
NEAR = NBS // 2


def iota(shape, dim):
    return lax.broadcasted_iota(jnp.int32, shape, dim)


def wide(row, rows=8):
    return jnp.broadcast_to(row, (rows, LANES))


def dense_tiles(quad, out_ref, v):
    comp = (iota((8, LANES), 1) // 8) % 4
    for b in range(4):
        rolled = [quad[k] if k == b else pltpu.roll(quad[k], ((k - b) * 8) % LANES, 1) for k in range(4)]
        row = jnp.where(
            comp < 2,
            jnp.where(comp == 0, rolled[0], rolled[1]),
            jnp.where(comp == 2, rolled[2], rolled[3]),
        )
        out_ref[pl.ds(pl.multiple_of(v * 32 + b * 8, 8), 8), :] = row


def lane_pick(planes, ids, beside):
    hi = [i >> 7 for i in ids]
    lo = [i & 127 for i in ids]
    out = [[jnp.zeros((8, LANES), F32)] * 4 for _ in ids]
    for r in range(LANES):
        same = [h == r for h in hi]
        for k in range(4):
            src = wide(planes[k, r : r + 1, :])
            for i in range(len(ids)):
                out[i][k] = jnp.where(same[i], jnp.take_along_axis(src, lo[i], axis=1), out[i][k])
        beside(r)
    return out


def fold8(parts):
    sub = iota((8, LANES), 0)
    for bit in (1, 2, 4):
        low = (sub & bit) == 0
        parts = [
            jnp.where(low, one, two) + pltpu.roll(jnp.where(low, two, one), bit, 0)
            for one, two in zip(parts[::2], parts[1::2])
        ]
    return parts[0]


def edge_distance(t, slab, other):
    above = other > slab
    shift = jnp.where(above, (other - slab) * NBS, (slab - other - 1) * NBS).astype(F32)
    slope = jnp.where(above, -1.0, 1.0).astype(F32)
    return shift + slope * t


def weight_of(n):
    return jnp.exp(-0.5 * (n + 0.5) * (n + 0.5))


def order_of(slab, lane, row):
    k = row * LANES + lane
    slab_k = k // NBS
    n = k % NBS
    ahead = jnp.where(slab_k > slab, n, NBS - 1 - n)
    own = jnp.where(n < NEAR, NEAR + n, NBS - 1 - n)
    back = jnp.where(n < NEAR, NBS - 1 - n, n - NEAR)
    steps = jnp.where(slab_k == slab, n % NEAR, n)
    to = lane - n + jnp.where(slab_k == slab, own, ahead)
    return to, lane - n + jnp.where(slab_k == slab, back, ahead), steps


def far_term(bins, mass, accs, slab, other, v):
    a = edge_distance(bins[v * 8 : v * 8 + 8, :], slab, other)
    q = jnp.exp(-a)
    term = mass[v * 8 : v * 8 + 8, :] * jnp.exp(-0.5 * a * (a + 1.0))
    for n in range(NBS):
        accs[n] = accs[n] + term
        if n < NBS - 1:
            term = term * q


def keep_bins(sums, slab, accs):
    at = pl.multiple_of(slab * NBS, NBS)
    sums[pl.ds(at, 8), :] = fold8(accs[:8])
    sums[pl.ds(at + 8, 8), :] = fold8(accs[8:])


def density(bins, mass, slab, sums, prof):
    accs = [jnp.zeros((8, LANES), F32)] * NBS
    for v in range(16):
        u = bins[v * 8 : v * 8 + 8, :] - NEAR
        for side, sign in ((0, 1.0), (1, -1.0)):
            q = jnp.exp(sign * u)
            term = mass[v * 8 : v * 8 + 8, :] * jnp.exp(-0.5 * u * (u - sign))
            for n in range(NEAR):
                accs[side * NEAR + n] = accs[side * NEAR + n] + term
                if n < NEAR - 1:
                    term = term * q
    keep_bins(sums, slab, accs)
    rows = []
    lane = iota((8, LANES), 1)
    for half in range(2):
        line = jnp.sum(sums[half * LANES : (half + 1) * LANES, :].T, axis=0, keepdims=True)
        _, source, steps = order_of(slab, lane, half)
        line = wide(line) * weight_of(steps.astype(F32))
        rows.append(jnp.take_along_axis(line, source, axis=1))
    sub = iota((8, LANES), 0)
    prof[...] = jnp.where(sub == 0, rows[0], jnp.where(sub == 1, rows[1], 0.0))


def site_tables(planes, tables):
    for i, k in enumerate((0, 1, 2, 4, 5)):
        turned = planes[k].T
        rest = jnp.concatenate([turned[:64], turned[64:]], axis=1)
        for part in range(3):
            term = rest.astype(jnp.bfloat16)
            tables[part, i * 64 : i * 64 + 64, :] = term
            rest = rest - term.astype(F32)


def member_sites(hyb_ref, tables, sites, m):
    rows = hyb_ref[pl.ds(m, 1), :]
    upper = ((rows >> 6) & 1) * LANES + (rows >> 7)
    hot = jnp.where(jnp.broadcast_to(upper, (256, 512)) == iota((256, 512), 0), 1.0, 0.0).astype(jnp.bfloat16)
    found = jnp.dot(tables[0], hot, preferred_element_type=F32)
    found = found + jnp.dot(tables[1], hot, preferred_element_type=F32)
    found = found + jnp.dot(tables[2], hot, preferred_element_type=F32)
    pick = jnp.broadcast_to(rows & 63, (64, 512)) == iota((64, 512), 0)
    for k in range(5):
        chosen = jnp.where(pick, found[k * 64 : k * 64 + 64], 0.0)
        total = sites[k]
        for j in range(8):
            total = total + chosen[j * 8 : j * 8 + 8]
        sites[k] = total


def coupling(mine, theirs, cols, pulls):
    for w in range(4):
        block = theirs[:, w * LANES : (w + 1) * LANES]
        cols[w * LANES : (w + 1) * LANES, :] = jnp.concatenate([block, jnp.zeros((LANES - 8, LANES), F32)], 0).T

    def step(r, accs):
        accs = list(accs)
        lot = cols[pl.ds(pl.multiple_of(r * 8, 8), 8), :]
        other = [jnp.broadcast_to(lot[:, k : k + 1], (8, LANES)) for k in range(5)]
        for w in range(4):
            own = [wide(mine[k : k + 1, w * LANES : (w + 1) * LANES]) for k in range(5)]
            d = [own[k] - other[k] for k in range(3)]
            near = 1.0 + (d[0] * d[0] + d[1] * d[1] + d[2] * d[2])
            weight = own[4] * other[4] * (own[3] + other[3]) / (near * near)
            for k in range(3):
                accs[w * 3 + k] = accs[w * 3 + k] + weight * d[k]
        return tuple(accs)

    accs = lax.fori_loop(0, 64, step, (jnp.zeros((8, LANES), F32),) * 12, unroll=8)
    for w in range(4):
        for k in range(3):
            pulls[k : k + 1, w * LANES : (w + 1) * LANES] = jnp.sum(accs[w * 3 + k], axis=0, keepdims=True) * (0.5 * 4.0 / 512)


def spread(pulls, hyb_ref, out):
    total = jnp.zeros((6 * LANES, LANES), F32)
    sub = iota((LANES, 512), 0)
    shares = []
    for k in range(3):
        share = pulls[k : k + 1, :] * 0.125
        high = share.astype(jnp.bfloat16).astype(F32)
        for part in (high, share - high):
            shares.append(jnp.broadcast_to(part, (LANES, 512)).astype(jnp.bfloat16))
    for m in range(8):
        rows = hyb_ref[m : m + 1, :]
        hit = jnp.broadcast_to(rows >> 7, (LANES, 512)) == sub
        lot = jnp.broadcast_to(rows & 127, (LANES, 512)) == sub
        hot = jnp.where(hit, 1.0, 0.0).astype(jnp.bfloat16)
        left = jnp.concatenate([hot * s for s in shares], 0)
        right = jnp.where(lot, 1.0, 0.0).astype(jnp.bfloat16)
        total = total + lax.dot_general(left, right, (((1,), (1,)), ((), ())), preferred_element_type=F32)
    for k in range(3):
        out[k] = total[2 * k * LANES : (2 * k + 1) * LANES] + total[(2 * k + 1) * LANES : (2 * k + 2) * LANES]


def comm_kernel(
    pos_hbm, zone_hbm, eps_hbm, mass_hbm, ghost_hbm, hyb_hbm, list_hbm,
    blocks_ref, prof_ref, spread_ref, local_ref, planes, rows_ref,
    zone_ref, mass_ref, ghost_ref, hyb_ref, bins, tables, sites,
    pay_ref, sums, part1, part2, got1, got2, mine, theirs, cols, pulls,
    load_sem, send_sem, recv_sem, s1, r1, s2, r2, ss, sr,
):
    group, slab_at, column = lax.axis_index("group"), lax.axis_index("gx"), lax.axis_index("yz")
    slab = group * 8 + slab_at

    loads = [
        pltpu.make_async_copy(src, dst, load_sem.at[i])
        for i, (src, dst) in enumerate((
            (pos_hbm, planes.at[0:3]), (zone_hbm, zone_ref), (eps_hbm, planes.at[5]),
            (ghost_hbm, ghost_ref), (mass_hbm, mass_ref), (hyb_hbm, hyb_ref), (list_hbm, rows_ref),
        ))
    ]
    for load in loads:
        load.start()

    def in_column(d):
        return (group, slab_at, lax.rem(column + d, 8))

    def across(d):
        return (lax.rem(group + d // 8, 2), lax.rem(slab_at + d % 8, 8), column)

    barrier = pltpu.get_barrier_semaphore()
    for d in range(1, 8):
        pl.semaphore_signal(barrier, inc=1, device_id=in_column(d), device_id_type=MESH)
    for d in range(1, 16):
        pl.semaphore_signal(barrier, inc=1, device_id=across(d), device_id_type=MESH)

    step = 512 // PIECES
    routes = (
        (1, None, across(1)),
        (7, None, across(7)),
        (3, None, in_column(1)),
        (5, None, in_column(7)),
        (0, 1, in_column(1)),
        (2, 1, in_column(7)),
        (6, 7, in_column(1)),
        (8, 7, in_column(7)),
    )

    def copy(index, p):
        block, source, target = routes[index]
        rows = pl.ds(p * step, step)
        src = pay_ref.at[rows] if source is None else blocks_ref.at[source, rows]
        return pltpu.make_async_remote_copy(
            src_ref=src, dst_ref=blocks_ref.at[block, rows],
            send_sem=send_sem.at[index, p], recv_sem=recv_sem.at[index, p],
            device_id=target, device_id_type=MESH,
        )

    def share1(d):
        return pltpu.make_async_remote_copy(
            src_ref=part1, dst_ref=got1.at[d], send_sem=s1.at[d], recv_sem=r1.at[d],
            device_id=in_column(d), device_id_type=MESH)

    def share2(d):
        return pltpu.make_async_remote_copy(
            src_ref=part2, dst_ref=got2.at[d], send_sem=s2.at[d], recv_sem=r2.at[d],
            device_id=across(d), device_id_type=MESH)

    def forward(p):
        for first, lot in ((0, (4, 5)), (1, (6, 7))):
            copy(first, p).wait_recv()
            for i in lot:
                copy(i, p).start()

    for i in range(3):
        loads[i].wait()

    def resolve(v, _):
        at = pl.ds(pl.multiple_of(v * 8, 8), 8)
        zone = zone_ref[at, :]
        lam = jnp.where(zone == 0, 1.0, jnp.where(zone == 1, jax.nn.sigmoid(2.0 * planes[0, at, :]), 0.0))
        planes[3, at, :] = planes[5, at, :] * jnp.where(group == 0, lam, 1.0 - lam)
        planes[4, at, :] = lam
        bins[at, :] = NBS * jax.nn.sigmoid(planes[0, at, :])
        return 0

    lax.fori_loop(0, 16, resolve, 0, unroll=4)
    site_tables(planes, tables)
    sites[...] = jnp.zeros_like(sites)
    for i in range(3, 6):
        loads[i].wait()
    pl.semaphore_wait(barrier, 22)

    def ghosts(v, _):
        ids = [ghost_ref[pl.ds(pl.multiple_of(v * 16 + 8 * i, 8), 8), :] for i in range(2)]
        index = [v * 2, jnp.minimum(v * 2 + 1, 14)]
        other = [i + (i >= slab).astype(jnp.int32) for i in index]
        accs = [jnp.zeros((8, LANES), F32)] * NBS

        def beside(r):
            if r % 4 == 0:
                far_term(bins, mass_ref, accs, slab, other[r // 64], r // 4 % 16)
            if r % 64 == 63:
                keep_bins(sums, other[r // 64], accs)
                accs[:] = [jnp.zeros((8, LANES), F32)] * NBS

        out = lane_pick(planes, ids, beside)
        member_sites(hyb_ref, tables, sites, v)
        for i in range(2):
            dense_tiles(out[i], pay_ref, v * 2 + i)
            at = pl.ds(pl.multiple_of(v * 16 + 8 * i, 8), 8)
            dense_tiles([planes[k, at, :] for k in range(4)], local_ref, v * 2 + i)

        @pl.when(v % 2 == 1)
        def _():
            for i in range(4):
                copy(i, v // 2).start()

        @pl.when((v % 2 == 1) & (v >= 5))
        def _():
            forward(v // 2 - 2)

        return 0

    lax.fori_loop(0, 8, ghosts, 0)
    loads[6].wait()
    tile = rows_ref[...]
    rows_ref[...] = (tile & -128) | ((tile & 3) << 5) | (((tile >> 2) & 3) << 3) | ((tile >> 4) & 7)
    mine[...] = jnp.zeros_like(mine)
    for k in range(5):
        mine[k : k + 1, :] = jnp.sum(sites[k], axis=0, keepdims=True) * 0.125
    swap = pltpu.make_async_remote_copy(
        src_ref=mine, dst_ref=theirs, send_sem=ss, recv_sem=sr, device_id=across(8), device_id_type=MESH)
    swap.start()
    density(bins, mass_ref, slab, sums, part1)
    for d in range(1, 8):
        share1(d).start()
    forward(PIECES - 2)
    swap.wait_recv()
    coupling(mine, theirs, cols, pulls)
    forward(PIECES - 1)
    for d in range(1, 8):
        share1(d).wait_recv()
    total = part1[...]
    for d in range(1, 8):
        total = total + got1[d]
    part2[...] = total
    for d in range(1, 16):
        share2(d).start()
    spread(pulls, hyb_ref, spread_ref)
    for d in range(1, 16):
        share2(d).wait_recv()
    total = part2[...]
    for d in range(1, 16):
        total = total + got2[d]
    prof_ref[...] = total
    for p in range(PIECES):
        for i in range(2, 8):
            copy(i, p).wait_recv()
    for p in range(PIECES):
        for i in range(8):
            copy(i, p).wait_send()
    for d in range(1, 8):
        share1(d).wait_send()
    for d in range(1, 16):
        share2(d).wait_send()
    swap.wait_send()


def force_kernel(
    nb_hbm, local_ref, blocks_ref, prof_ref, spread_ref, planes,
    out_ref,
    nb_ref, table, turned, gathered, lots, forces, push, coef_a, coef_b, load_sem,
):
    group = lax.axis_index("group")
    slab = group * 8 + lax.axis_index("gx")
    load = pltpu.make_async_copy(nb_hbm, nb_ref, load_sem.at[0])
    load.start()
    lane = iota((8, LANES), 1)
    quarter = lane // 32

    def fill(source, block):
        def one(r, _):
            for u in range(16):
                rows = source[pl.ds(pl.multiple_of(r * 128 + u * 8, 8), 8), :]
                rolled = [rows] + [pltpu.roll(rows, 32 * k, 1) for k in (1, 2, 3)]
                at = pl.multiple_of(block * 2048 + r * 512 + u * 32, 8)
                for q in range(4):
                    tile = jnp.where(
                        quarter < 2,
                        jnp.where(quarter == 0, rolled[-q % 4], rolled[(1 - q) % 4]),
                        jnp.where(quarter == 2, rolled[(2 - q) % 4], rolled[(3 - q) % 4]),
                    )
                    table[pl.ds(at + q * 8, 8), :] = tile
            return 0

        lax.fori_loop(0, 4, one, 0)

    fill(local_ref, 0)

    def ghost_fill(index, _):
        block = index + (index >= 4).astype(jnp.int32)
        fill(blocks_ref.at[block], block + 1)
        return 0

    lax.fori_loop(0, 8, ghost_fill, 0)
    table[20480:20488, :] = jnp.zeros((8, LANES), F32)
    for k in range(4):
        turned[k] = planes[k].T

    profile = prof_ref[...]
    mean = jnp.sum(profile) / 256.0
    for half in range(2):
        source, _, steps = order_of(slab, lane, half)
        steps = steps.astype(F32)
        dev = wide(profile[half : half + 1, :] / mean - 1.0)
        dev = jnp.take_along_axis(dev, source, axis=1) * weight_of(steps)
        coef_a[half * LANES : (half + 1) * LANES, :] = wide(dev[0:1, :], LANES).T
        coef_b[half * LANES : (half + 1) * LANES, :] = wide((dev * steps)[0:1, :], LANES).T

    def horner(q, start, count):
        a = wide(coef_a[pl.ds(start + count - 1, 1), :])
        b = wide(coef_b[pl.ds(start + count - 1, 1), :])
        for n in range(count - 2, -1, -1):
            a = a * q + wide(coef_a[pl.ds(start + n, 1), :])
            b = b * q + wide(coef_b[pl.ds(start + n, 1), :])
        return a, b

    def thermo_part(t, index):
        if index < 15:
            other = index + (index >= slab).astype(jnp.int32)
            dist = edge_distance(t, slab, other)
            a, b = horner(jnp.exp(-dist), other * NBS, NBS)
            part = jnp.exp(-0.5 * dist * (dist + 1.0)) * ((dist + 0.5) * a + b)
            return jnp.where(other > slab, -part, part)
        u = t - NEAR
        a, b = horner(jnp.exp(u), slab * NBS, NEAR)
        upper = jnp.exp(-0.5 * u * (u - 1.0)) * ((u - 0.5) * a - b)
        a, b = horner(jnp.exp(-u), slab * NBS + NEAR, NEAR)
        return upper + jnp.exp(-0.5 * u * (u + 1.0)) * ((u + 0.5) * a + b)

    def take(slot, cl):
        g = slot % 4
        for c in range(LANES):
            flat = (slot // 8) * 16384 + (c // 8) * 1024 + (slot % 8) * 128 + (c % 8) * 16
            tile = nb_ref.at[pl.ds(flat, 16)][cl]
            gathered[slot // 4, c : c + 1, 32 * g : 32 * g + 32] = table[pl.ds(tile, 1), 32 * g : 32 * g + 32]

    def pairs(curve, i, cl, slots, total):
        own = [wide(turned[k, pl.ds(cl * 8 + i, 1), :]) for k in range(3)]
        for slot in slots:
            quad, g = slot // 4, slot % 4
            at = [lots[quad, 32 * g + 8 * k : 32 * g + 8 * k + 8, :] for k in range(4)]
            d = [own[k] - at[k] for k in range(3)]
            w = at[3] * curve(d[0] * d[0] + d[1] * d[1] + d[2] * d[2])
            total = [total[k] + w * d[k] for k in range(3)]
        return total

    def keep(cl, accs):
        at = pl.ds(pl.multiple_of(cl * 8, 8), 8)
        charge = turned[3, at, :]
        for k in range(3):
            forces[k, at, :] = charge * fold8([acc[k] for acc in accs])

    def run(curve):
        zero = [jnp.zeros((8, LANES), F32)] * 3

        def body(cl, _):
            for quad in range(4):
                lots[quad] = gathered[quad].T
            before = jnp.maximum(cl - 1, 0)
            at = pl.ds(pl.multiple_of(cl * 8, 8), 8)
            t = NBS * jax.nn.sigmoid(planes[0, at, :])
            push_sum = jnp.zeros((8, LANES), F32)
            accs = [zero] * 8
            for slot in range(16):
                i, first = slot // 2, slot % 2 * 8
                accs[i] = pairs(curve, i, before, range(first, first + 8), accs[i])
                push_sum = push_sum + thermo_part(t, slot)
                take(slot, cl)
            lam = planes[4, at, :]
            push[at, :] = -4.0 * lam * (1.0 - lam) * push_sum
            keep(before, accs)
            return 0

        lax.fori_loop(0, 16, body, 0)
        for quad in range(4):
            lots[quad] = gathered[quad].T
        keep(15, [pairs(curve, i, 15, range(16), zero) for i in range(8)])

    def soft(s):
        near = 1.0 + s
        r = pl.reciprocal(near, approx=True)
        r = r * (2.0 - near * r)
        return r * r * r

    gathered[...] = jnp.zeros_like(gathered)
    load.wait()

    @pl.when(group == 0)
    def _():
        run(soft)

    @pl.when(group != 0)
    def _():
        run(lambda s: jnp.exp(-0.5 * s))

    for k in range(3):
        plane = forces[k].T + spread_ref[k]
        if k == 0:
            plane = plane + push[...]
        out_ref[k] = plane


VMEM = pl.BlockSpec(memory_space=pltpu.VMEM)
ANY = pl.BlockSpec(memory_space=pl.ANY)
HBM = pl.BlockSpec(memory_space=pltpu.HBM)


def shape(*dims):
    return jax.ShapeDtypeStruct(dims, F32)


def per_device(site_pos, zone_id, site_eps, site_mass, neighbours, ghost_rows, hyb_map):
    pos = site_pos.reshape(3, 128, 128)
    zone = zone_id.reshape(128, 128)
    eps = site_eps.reshape(128, 128)
    mass = site_mass.reshape(128, 128)
    lists = neighbours.reshape(2, 8, 16, 128).transpose(0, 2, 1, 3).reshape(256, 128)
    ghost = ghost_rows.reshape(128, 128)
    hyb = hyb_map.reshape(8, 512)
    blocks, prof, extra, local, state, rows = pl.pallas_call(
        comm_kernel,
        out_shape=(shape(9, 512, 128), shape(8, 128), shape(3, 128, 128), shape(512, 128), shape(6, 128, 128), jax.ShapeDtypeStruct((256, 128), jnp.int32)),
        in_specs=[HBM] * 7,
        out_specs=(ANY, VMEM, VMEM, VMEM, VMEM, VMEM),
        scratch_shapes=[
            pltpu.VMEM((128, 128), jnp.int32),
            pltpu.VMEM((128, 128), F32),
            pltpu.VMEM((128, 128), jnp.int32),
            pltpu.VMEM((8, 512), jnp.int32),
            pltpu.VMEM((128, 128), F32),
            pltpu.VMEM((3, 320, 256), jnp.bfloat16),
            pltpu.VMEM((5, 8, 512), F32),
            pltpu.VMEM((512, 128), F32),
            pltpu.VMEM((256, 128), F32),
            pltpu.VMEM((8, 128), F32),
            pltpu.VMEM((8, 128), F32),
            pltpu.VMEM((8, 8, 128), F32),
            pltpu.VMEM((16, 8, 128), F32),
            pltpu.VMEM((8, 512), F32),
            pltpu.VMEM((8, 512), F32),
            pltpu.VMEM((512, 128), F32),
            pltpu.VMEM((8, 512), F32),
            pltpu.SemaphoreType.DMA((7,)),
            pltpu.SemaphoreType.DMA((8, PIECES)),
            pltpu.SemaphoreType.DMA((8, PIECES)),
            pltpu.SemaphoreType.DMA((8,)),
            pltpu.SemaphoreType.DMA((8,)),
            pltpu.SemaphoreType.DMA((16,)),
            pltpu.SemaphoreType.DMA((16,)),
            pltpu.SemaphoreType.DMA,
            pltpu.SemaphoreType.DMA,
        ],
        compiler_params=pltpu.CompilerParams(
            collective_id=0, has_side_effects=True, vmem_limit_bytes=62 * 2**20
        ),
        name="exchange",
    )(pos, zone, eps, mass, ghost, hyb, lists)
    forces = pl.pallas_call(
        force_kernel,
        out_shape=shape(3, 128, 128),
        in_specs=[HBM, VMEM, VMEM, VMEM, VMEM, VMEM],
        out_specs=VMEM,
        scratch_shapes=[
            pltpu.SMEM((32768,), jnp.int32),
            pltpu.VMEM((20488, 128), F32),
            pltpu.VMEM((4, 128, 128), F32),
            pltpu.VMEM((4, 128, 128), F32),
            pltpu.VMEM((4, 128, 128), F32),
            pltpu.VMEM((3, 128, 128), F32),
            pltpu.VMEM((128, 128), F32),
            pltpu.VMEM((256, 128), F32),
            pltpu.VMEM((256, 128), F32),
            pltpu.SemaphoreType.DMA((1,)),
        ],
        compiler_params=pltpu.CompilerParams(vmem_limit_bytes=56 * 2**20),
        name="forces",
    )(rows.reshape(32768), local, blocks, prof, extra, state)
    return forces.reshape(1, 1, 1, 3, 16384)


def solution(mesh):
    return jax.shard_map(
        per_device,
        mesh=mesh,
        in_specs=(
            P("group", "gx", "yz", None, None),
            P("group", "gx", "yz", None),
            P("group", "gx", "yz", None),
            P("group", "gx", "yz", None),
            P("group", "gx", "yz", None, None),
            P("group", "gx", "yz", None),
            P("group", "gx", "yz", None, None),
        ),
        out_specs=P("group", "gx", "yz", None, None),
        check_vma=False,
    )
```
